512 devices in a mesh: seq: 32 (over z, x_hi), mp: 16 (over x_lo, y, core).
Axes of the slice: x: 4 (x_hi: 2, x_lo: 2; x = x_hi * 2 + x_lo), y: 4, z: 16, core: 2. Of those that a mesh axis runs over, the one named last changes fastest.
Arguments:
- queries: bfloat16 [4096, 4096], P('seq', 'mp'), may hold values from -100 to 100
- stretch_keys: bfloat16 [4096, 4096], P('seq', 'mp'), may hold values from -6 to 6
- stretch_values: bfloat16 [4096, 4096], P('seq', 'mp'), may hold values from -5 to 5
- cache_keys: bfloat16 [4096, 4096], P('seq', 'mp'), may hold values from -5 to 5
- cache_values: bfloat16 [4096, 4096], P('seq', 'mp'), may hold values from -5 to 5
- cache_lengths: int32 [32], P('seq'), may hold values from 1 to 128, as said below
- frame_mask: int32 [4, 4], replicated, may hold values from 0 to 1, as said below
- out_weight: bfloat16 [4096, 5120], P('mp'), may hold values from -0.09375 to 0.09375
- head_weight: bfloat16 [5120, 64], P('mp'), may hold values from -0.8359375 to 0.8359375
- previous_latent: bfloat16 [2, 32, 128, 16], P(None, 'mp', 'seq'), may hold values from -2 to 2
- conv_weight: bfloat16 [3, 3, 3, 16, 384], replicated, may hold values from -0.3125 to 0.3125
- conv_bias: float32 [384], replicated, may hold values from -1.5 to 1.5
- norm_gain: float32 [384], replicated, may hold values from 0.5 to 1.5
Outputs:
- decoded: bfloat16 [4, 32, 128, 384], P(None, 'mp', 'seq')
The draws below stay inside these ranges and needn't reach their ends.
Inputs may be any that keep to these rules, and one draw needn't show every extreme that they name: `cache_lengths`: some index of seq has all 128 slots filled. `frame_mask`: the diagonal is 1 and the entries above it are 0.
All inputs are finite; a program needn't handle non-finite values.
Results may differ from the reference program's by a relative error of at most 0.034.
Values may be sent and summed in bfloat16 or wider, within the bound.
No kernel may reach another device: no remote copies, remote signals or barrier semaphores. Data moves between devices by JAX's collectives and lax.ppermute only.
A program may use at most 64 MiB of HBM per device.

```python
import math
import jax
import jax.numpy as jnp
from jax import lax

HD = 128
HEADS = 32
DM = 5120
LATC = 16
CH = 384
FR = 4
CACHE_DEV = 128
TOKENS = 4096
CACHE = 4096
PW = 64
PH = 16
N_SEQ = 32


def shared_keys(key):
    field = jax.random.normal(jax.random.fold_in(key, 101), (TOKENS, HEADS * HD), jnp.float32)
    return jnp.clip(field, -4.0, 4.0)


def draw_queries(key, part):
    key = jax.random.fold_in(key, 3)
    field = jnp.clip(jax.random.normal(key, (TOKENS, HEADS * HD), jnp.float32), -4.0, 4.0)
    return field.astype(jnp.bfloat16)


def draw_stretch_keys(key, part):
    base = shared_keys(key)
    return base.astype(jnp.bfloat16)


def draw_frame_mask(key, part):
    key = jax.random.fold_in(key, 5)
    coins = jax.random.randint(key, (FR, FR), 0, 2).astype(jnp.int32)
    lower = jnp.arange(FR)[:, None] > jnp.arange(FR)[None, :]
    diag = jnp.arange(FR)[:, None] == jnp.arange(FR)[None, :]
    return (jnp.where(lower, coins, 0) + diag.astype(jnp.int32)).astype(jnp.int32)


def draw_cache_lengths(key, part):
    key = jax.random.fold_in(key, 7)
    lengths = jax.random.randint(jax.random.fold_in(key, 1), (N_SEQ,), 1, CACHE_DEV + 1)
    fullone = jax.random.randint(jax.random.fold_in(key, 2), (), 0, N_SEQ)
    return jnp.where(jnp.arange(N_SEQ) == fullone, CACHE_DEV, lengths).astype(jnp.int32)


def levels(rng, extent, cuts, least, largest):
    gain, own = 1.0, jax.random.fold_in(rng, 6)
    for axis_at, shards_of in cuts:
        steps = jnp.exp(jax.random.uniform(jax.random.fold_in(own, axis_at), (shards_of,), jnp.float32, least / len(cuts), largest / len(cuts)))
        gain = gain * jnp.repeat(steps, extent[axis_at] // shards_of).reshape([-1 if axis == axis_at else 1 for axis in range(len(extent))])
    return gain


def centred(key, extent, spread, most, cuts=(), kind=jnp.bfloat16):
    factor_of = levels(key, extent, cuts, -0.22, 0.18) if cuts else 1.0
    drawn = jax.random.normal(key, extent, jnp.float32) * spread * factor_of
    return jnp.minimum(jnp.maximum(drawn, -most), most).astype(kind)


def setup_inputs(seed: int = 0) -> dict:
    keys = jax.random.split(jax.random.key(seed), 14)
    queries = draw_queries(jax.random.fold_in(keys[13], 71), 0)
    stretch_keys = draw_stretch_keys(jax.random.fold_in(keys[13], 71), 0)
    stretch_values = centred(keys[2], (TOKENS, HEADS * HD), 1.0, 5.0, ((0, 32), (1, 16)))
    cache_keys = centred(keys[3], (CACHE, HEADS * HD), 1.0, 5.0, ((0, 32), (1, 16)))
    cache_values = centred(keys[4], (CACHE, HEADS * HD), 1.0, 5.0, ((0, 32), (1, 16)))
    cache_lengths = draw_cache_lengths(jax.random.fold_in(keys[13], 71), 0)
    frame_mask = draw_frame_mask(jax.random.fold_in(keys[13], 71), 0)
    out_weight = centred(keys[7], (HEADS * HD, DM), (HEADS * HD) ** -0.5, 0.09375, ((0, 16),))
    head_weight = centred(keys[8], (DM, 4 * LATC), (12.0 / DM ** 0.5), 0.8359375, ((0, 16),))
    previous_latent = centred(keys[9], (2, 2 * PH, 2 * PW, LATC), 0.3, 2.0, ((1, 16), (2, 32)))
    conv_weight = centred(keys[10], (3, 3, 3, LATC, CH), (27 * LATC) ** -0.5, 0.3125)
    conv_bias = centred(keys[11], (CH,), 0.3, 1.5, (), jnp.float32)
    norm_gain = jnp.clip(1.0 + 0.1 * jax.random.normal(keys[12], (CH,), jnp.float32), 0.5, 1.5)
    return {"queries": queries, "stretch_keys": stretch_keys, "stretch_values": stretch_values, "cache_keys": cache_keys, "cache_values": cache_values, "cache_lengths": cache_lengths, "frame_mask": frame_mask, "out_weight": out_weight, "head_weight": head_weight, "previous_latent": previous_latent, "conv_weight": conv_weight, "conv_bias": conv_bias, "norm_gain": norm_gain}


def reference(queries, stretch_keys, stretch_values, cache_keys, cache_values, cache_lengths, frame_mask, out_weight, head_weight, previous_latent, conv_weight, conv_bias, norm_gain):
    tokens = queries.shape[0]
    heads = queries.shape[1] // HD
    scale = 1.0 / math.sqrt(HD)
    frames = (jnp.arange(tokens) // (tokens // FR)).astype(jnp.int32)
    vis_stretch = frame_mask[frames[:, None], frames[None, :]] == 1
    cache_rows = cache_keys.shape[0]
    owner = (jnp.arange(cache_rows) // CACHE_DEV).astype(jnp.int32)
    vis_cache = (jnp.arange(cache_rows) % CACHE_DEV).astype(jnp.int32) < cache_lengths[owner]

    def split(field):
        return field.reshape(field.shape[0], heads, HD).transpose(1, 0, 2)

    def one_head(group):
        query, key_cache, val_cache, key_stretch, val_stretch = group
        score_cache = jnp.dot(query, key_cache.T, preferred_element_type=jnp.float32) * scale
        score_stretch = jnp.dot(query, key_stretch.T, preferred_element_type=jnp.float32) * scale
        score_cache = jnp.where(vis_cache[None, :], score_cache, -1e+30)
        score_stretch = jnp.where(vis_stretch, score_stretch, -1e+30)
        top = jnp.maximum(lax.optimization_barrier(jnp.max(score_cache, 1)), lax.optimization_barrier(jnp.max(score_stretch, 1)))[:, None]
        weight_cache = jnp.where(vis_cache[None, :], jnp.exp(score_cache - top), 0.0)
        weight_stretch = jnp.where(vis_stretch, jnp.exp(score_stretch - top), 0.0)
        total = lax.optimization_barrier(jnp.sum(weight_cache, 1)) + lax.optimization_barrier(jnp.sum(weight_stretch, 1))
        summed = jnp.dot(weight_cache.astype(jnp.bfloat16), val_cache, preferred_element_type=jnp.float32)
        summed = summed + jnp.dot(weight_stretch.astype(jnp.bfloat16), val_stretch, preferred_element_type=jnp.float32)
        return (summed / total[:, None]).astype(jnp.bfloat16)
    attended = lax.map(one_head, (split(queries), split(cache_keys), split(cache_values), split(stretch_keys), split(stretch_values)))
    attended = attended.transpose(1, 0, 2).reshape(tokens, heads * HD)
    projected = jnp.dot(attended, out_weight, preferred_element_type=jnp.float32).astype(jnp.bfloat16)
    latent = jnp.dot(projected, head_weight, preferred_element_type=jnp.float32).astype(jnp.bfloat16)
    pixels = latent.reshape(FR, PH, PW, 2, 2, LATC).transpose(0, 1, 3, 2, 4, 5).reshape(FR, 2 * PH, 2 * PW, LATC)
    stacked = jnp.concatenate([previous_latent, pixels], 0)
    padded = jnp.pad(stacked, ((0, 0), (1, 1), (1, 1), (0, 0)))
    pieces = []
    for step_t in range(3):
        for step_y in range(3):
            for step_x in range(3):
                pieces.append(padded[step_t:step_t + FR, step_y:step_y + 2 * PH, step_x:step_x + 2 * PW, :])
    columns = jnp.stack(pieces, 3).reshape(-1, 27 * LATC)
    conv = jnp.dot(columns, conv_weight.reshape(27 * LATC, CH), preferred_element_type=jnp.float32) + conv_bias
    meansq = lax.optimization_barrier(jnp.mean(conv * conv, -1, keepdims=True))
    normed = conv * lax.rsqrt(meansq + 1e-06) * norm_gain
    return jax.nn.silu(normed).astype(jnp.bfloat16).reshape(FR, 2 * PH, 2 * PW, CH)
```

```python
import math

import jax
import jax.numpy as jnp
import numpy as np
from jax import lax
from jax.experimental import pallas as pl
from jax.experimental.pallas import tpu as pltpu
from jax.sharding import Mesh, PartitionSpec as P

HD = 128
LATC = 16
CH = 384
FR = 4
NZ = 16
NEG = -1e30
C2 = math.log2(math.e) / math.sqrt(HD)
F32 = jnp.float32
BF16 = jnp.bfloat16
FAR = [[(4 * j + i) * 2 + k for j in range(4) for k in range(2)] for i in range(4)]
NEAR = [[(4 * i + j) * 2 + k for j in range(4) for k in range(2)] for i in range(4)]
NT = (((1,), (1,)), ((), ()))


def dot_nt(a, b):
    return lax.dot_general(a, b, NT, preferred_element_type=F32)


def attend_kernel(fm_ref, pos_ref, q_ref, kv_ref, w2t_ref, pv_ref, out_ref, pt_ref):
    group = pos_ref[0] // 4
    lane = lax.broadcasted_iota(jnp.int32, (1, HD), 1)
    row_frame = lax.broadcasted_iota(jnp.int32, (128, 1), 0) // 32
    block_bias = jnp.zeros((128, 1), F32)
    for f in range(FR):
        here = jnp.where(fm_ref[f, group] == 1, 0.0, NEG)
        block_bias = jnp.where(row_frame == f, here, block_bias)
    block_bias = jnp.broadcast_to(block_bias, (128, 128))
    cache_bias = []
    for s in range(8):
        filled = kv_ref[s, 512:528, :].astype(F32)[0:1]
        cache_bias.append(jnp.where(lane.astype(F32) < filled, 0.0, NEG))

    def block(b, carry):
        q = q_ref[:, b].reshape(128, HD)
        scores = []
        for s in range(8):
            raw = dot_nt(q, kv_ref[s, 0:256, :]) * C2
            bias = jnp.concatenate(
                [jnp.broadcast_to(cache_bias[s], (128, 128)), block_bias], axis=1
            )
            scores.append(raw + bias)
        top = scores[0]
        for s in range(1, 8):
            top = jnp.maximum(top, scores[s])
        top = jnp.max(top, axis=1, keepdims=True)
        total = jnp.zeros((128, 256), F32)
        acc = jnp.zeros((128, HD), F32)
        for s in range(8):
            weights = jnp.exp2(scores[s] - top)
            total = total + weights
            acc = acc + jnp.dot(
                weights.astype(BF16), kv_ref[s, 256:512, :], preferred_element_type=F32
            )
        total = jnp.sum(total, axis=1, keepdims=True)
        attended = (acc / total).astype(BF16)
        pt_ref[b, 0:64] = dot_nt(w2t_ref[...], attended)
        level = jnp.broadcast_to(top + jnp.log2(total), (128, 128)).T[0:8]
        high = level.astype(BF16).astype(F32)
        mid = (level - high).astype(BF16).astype(F32)
        low = level - high - mid
        part = lax.broadcasted_iota(jnp.int32, (8, 128), 0)
        pt_ref[b, 64:72] = jnp.where(
            part == 0, high, jnp.where(part == 1, mid, jnp.where(part == 2, low, 0.0))
        )
        return carry

    lax.fori_loop(0, 8, block, 0)
    column = lax.broadcasted_iota(jnp.int32, (72, 128), 1) % 8
    for z in range(NZ):
        b = z // 2
        own = pt_ref[b]
        if z % 2 == 0:
            chunk = jnp.where(column <= 4, own, 0.0)
            if b > 0:
                chunk = jnp.where(column == 7, pt_ref[b - 1], chunk)
        else:
            chunk = jnp.where(column >= 3, own, 0.0)
            if b < 7:
                chunk = jnp.where(column == 0, pt_ref[b + 1], chunk)
        out_ref[z, 0:64] = chunk[0:64].astype(BF16)
        out_ref[z, 64:80] = jnp.concatenate([chunk[64:72], pv_ref[...]], axis=0).astype(BF16)


def spread_kernel(pos_ref, y_ref, pv_ref, pick_ref, out_ref, rhs_ref):
    z, h, m = pos_ref[0], pos_ref[1], pos_ref[2]
    odd = z % 2 == 1
    column = lax.broadcasted_iota(jnp.int32, (64, 128), 1) % 8
    rhs_ref[...] = jnp.zeros_like(rhs_ref)
    for r in range(4):
        levels = []
        for g in range(4):
            tail = y_ref[4 * g + r, 64:80].astype(F32)
            levels.append(tail[0:1] + tail[1:2] + tail[2:3])
        top = jnp.maximum(jnp.maximum(levels[0], levels[1]), jnp.maximum(levels[2], levels[3]))
        shares = [jnp.exp2(level - top) for level in levels]
        whole = shares[0] + shares[1] + shares[2] + shares[3]
        value = jnp.zeros((64, 128), F32)
        for g in range(4):
            value = value + (shares[g] / whole) * y_ref[4 * g + r, 0:64].astype(F32)
        turned = jnp.where(
            column < 4, pltpu.roll(value, 124, 1), pltpu.roll(value, 4, 1)
        )
        value = jnp.where(odd, turned, value)
        rhs_ref[0:64, 128 * r : 128 * r + 128] = value.astype(BF16)
    left = y_ref[jnp.maximum(z - 1, 0), 64:80].astype(F32)[8:16]
    right = y_ref[jnp.minimum(z + 1, NZ - 1), 64:80].astype(F32)[8:16]
    left = jnp.where((z > 0) & (h == 1), left, 0.0)
    right = jnp.where((z < NZ - 1) & (h == 0), right, 0.0)
    rows = jnp.concatenate([pv_ref[...], left, right], axis=0)[:, 0:64].astype(BF16)
    item = lax.broadcasted_iota(jnp.int32, (24, 256), 0)
    spot = lax.broadcasted_iota(jnp.int32, (24, 256), 1)
    kind, index = item // 8, item % 8
    patch, frame = index // 2, index % 2
    cell = jnp.where(kind == 0, 2 * h + patch, jnp.where(kind == 1, 7, 4))
    wanted = (kind == 0) & (patch < 2) | (kind == 1) & (patch == 1) | (kind == 2) & (patch == 0)
    place = wanted & (spot // 128 == frame) & ((spot // 8) % 16 == m) & (spot % 8 == cell)
    place = jnp.where(place, 1.0, 0.0).astype(BF16)
    moved = lax.dot_general(rows, place, (((0,), (0,)), ((), ())), preferred_element_type=F32)
    rhs_ref[64:128, 512:768] = moved.astype(BF16)
    for part in range(4):
        got = dot_nt(pick_ref[384 * part : 384 * part + 384, :], rhs_ref[...])
        out_ref[8 * part : 8 * part + 8] = got.astype(BF16).reshape(8, 48, 128)


def picks():
    pick = np.zeros((2, 16, 3, 4, 4, 768), np.float32)
    cells = ((7, 0, 1, 2), (1, 2, 3, 4))
    for h in range(2):
        for m in range(16):
            for dr in range(3):
                row = m + dr - 1
                if not 0 <= row < 16:
                    continue
                for cc in range(4):
                    c = cells[h][cc]
                    for f in range(4):
                        pick[h, m, dr, cc, f, (row // 4) * 128 + f * 32 + (row % 4) * 8 + c] = 1
                        if f < 2:
                            pick[h, m, dr, cc, f, 512 + f * 128 + row * 8 + c] = 1
    return pick.reshape(1536, 768)


def decode_kernel(r_ref, w_ref, bias_ref, gain_ref, out_ref, z_ref):
    total = jnp.zeros((48, 128), F32)
    for s in range(32):
        total = total + r_ref[s].astype(F32)
    total = total.astype(BF16).astype(F32)
    z_ref[...] = jnp.zeros_like(z_ref)
    for dr in range(3):
        for cc in range(4):
            at = dr * 16 + cc * 4
            z_ref[dr, cc * 6 + 2 : cc * 6 + 6] = total[at : at + 4, 0:64]
            z_ref[dr, cc * 6 : cc * 6 + 2] = total[at : at + 2, 64:128]
    for a in range(2):
        for b in range(2):
            conv = jnp.zeros((16, CH), F32)
            for dt in range(3):
                pieces = []
                for i in range(2):
                    for j in range(2):
                        start = (b + j) * 6 + dt
                        pieces.append(z_ref[a + i, start : start + 16])
                lhs = jnp.concatenate(pieces, axis=1).astype(BF16)
                conv = conv + jnp.dot(lhs, w_ref[a, b, dt], preferred_element_type=F32)
            conv = conv + bias_ref[...]
            meansq = jnp.mean(conv * conv, axis=1, keepdims=True)
            normed = conv * lax.rsqrt(meansq + 1e-06) * gain_ref[...]
            decoded = (normed / (1.0 + jnp.exp(-normed))).astype(BF16)
            for c in range(2):
                for f in range(FR):
                    out_ref[f, a, 2 * c + b] = decoded[c * 6 + f]


def body(
    queries,
    stretch_keys,
    stretch_values,
    cache_keys,
    cache_values,
    cache_lengths,
    frame_mask,
    out_weight,
    head_weight,
    previous_latent,
    conv_weight,
    conv_bias,
    norm_gain,
):
    z, h, m = lax.axis_index("z"), lax.axis_index("h"), lax.axis_index("mp")
    pos = jnp.stack([z, h, m]).astype(jnp.int32)
    vmem = pl.BlockSpec(memory_space=pltpu.VMEM)
    smem = pl.BlockSpec(memory_space=pltpu.SMEM)
    params = pltpu.CompilerParams(vmem_limit_bytes=40 * 1024 * 1024)

    q = queries.reshape(2, 8, 8, 2, HD).transpose(3, 1, 0, 2, 4).reshape(1, 2, 8, 16, HD)
    q = jnp.broadcast_to(q, (4, 2, 8, 16, HD)).reshape(8, 8, 16, HD)
    q = lax.all_to_all(q, ("z", "h"), 0, 0, tiled=True, axis_index_groups=FAR)
    filled = jnp.broadcast_to(cache_lengths[0].astype(BF16), (16, 2 * HD))
    kv = jnp.concatenate([cache_keys, stretch_keys, cache_values, stretch_values, filled], 0)
    kv = kv.reshape(1, 528, 2, HD).transpose(0, 2, 1, 3)
    kv = jnp.broadcast_to(kv, (4, 2, 528, HD)).reshape(8, 528, HD)
    kv = lax.all_to_all(kv, ("z", "h"), 0, 0, tiled=True, axis_index_groups=NEAR)
    hw = jnp.broadcast_to(head_weight[None], (16,) + head_weight.shape)
    hw = lax.all_to_all(hw, "mp", 0, 0, tiled=True).reshape(-1, 64)
    rows = lax.dynamic_slice_in_dim(out_weight, h * HD, HD, 0)
    w2t = lax.dot_general(
        hw, rows, (((0,), (1,)), ((), ())), preferred_element_type=F32
    ).astype(BF16)
    pv = previous_latent.reshape(2, 2, 2, 2, LATC).transpose(2, 0, 1, 3, 4).reshape(4, 64)
    pv = jnp.pad(pv.astype(F32), ((0, 4), (0, 64)))

    partial = pl.pallas_call(
        attend_kernel,
        out_shape=jax.ShapeDtypeStruct((NZ, 80, 128), BF16),
        in_specs=[smem, smem, vmem, vmem, vmem, vmem],
        out_specs=vmem,
        scratch_shapes=[pltpu.VMEM((8, 72, 128), F32)],
        compiler_params=params,
        name="attend",
    )(frame_mask, pos, q, kv, w2t, pv)
    partial = lax.all_to_all(partial, "z", 0, 0, tiled=True)
    spread = pl.pallas_call(
        spread_kernel,
        out_shape=jax.ShapeDtypeStruct((32, 48, 128), BF16),
        in_specs=[smem, vmem, vmem, vmem],
        out_specs=vmem,
        scratch_shapes=[pltpu.VMEM((128, 768), BF16)],
        compiler_params=params,
        name="spread",
    )(pos, partial, pv, jnp.asarray(picks(), BF16))
    spread = lax.all_to_all(spread, ("h", "mp"), 0, 0, tiled=True)
    taps = []
    for a in range(2):
        for b in range(2):
            w = jnp.pad(conv_weight, ((0, 0), (1 - a, a), (1 - b, b), (0, 0), (0, 0)))
            w = w.reshape(3, 2, 2, 2, 2, LATC, CH).transpose(0, 1, 3, 2, 4, 5, 6)
            taps.append(w.reshape(3, 256, CH))
    taps = jnp.stack(taps).reshape(2, 2, 3, 256, CH)
    return pl.pallas_call(
        decode_kernel,
        out_shape=jax.ShapeDtypeStruct((FR, 2, 4, CH), BF16),
        in_specs=[vmem] * 4,
        out_specs=vmem,
        scratch_shapes=[pltpu.VMEM((3, 40, 64), F32)],
        compiler_params=params,
        name="decode",
    )(spread, taps, conv_bias.reshape(1, CH), norm_gain.reshape(1, CH))


def solution(mesh):
    fine = Mesh(mesh.devices.reshape(NZ, 2, 16), ("z", "h", "mp"))
    seq = ("z", "h")
    return jax.shard_map(
        body,
        mesh=fine,
        in_specs=(
            P(seq, "mp"),
            P(seq, "mp"),
            P(seq, "mp"),
            P(seq, "mp"),
            P(seq, "mp"),
            P(seq),
            P(),
            P("mp", None),
            P("mp", None),
            P(None, "mp", seq, None),
            P(),
            P(),
            P(),
        ),
        out_specs=P(None, "mp", seq, None),
        check_vma=False,
    )
```

```python
import functools
import math

import jax
import jax.numpy as jnp
from jax import lax
from jax.experimental import pallas as pl
from jax.experimental.pallas import tpu as pltpu
from jax.sharding import Mesh, PartitionSpec as P

HD = 128
LATC = 16
CH = 384
FR = 4
NZ = 16
NEG = -1e30
C2 = math.log2(math.e) / math.sqrt(HD)
F32 = jnp.float32
BF16 = jnp.bfloat16
FAR = [[(4 * j + i) * 2 + k for j in range(4) for k in range(2)] for i in range(4)]
NT = (((1,), (1,)), ((), ()))


def dot_nt(a, b):
    return lax.dot_general(a, b, NT, preferred_element_type=F32)


def pack_kernel(
    h, len_ref, q_hbm, ck_hbm, sk_hbm, cv_hbm, sv_hbm, keep_ref, give_ref, qo_ref, buf, sems
):
    copies = []
    for n, ref in enumerate((ck_hbm, sk_hbm, cv_hbm, sv_hbm, q_hbm)):
        copies.append(pltpu.make_async_copy(ref, buf.at[n], sems.at[n]))
        copies[n].start()
    first = h[0] == 0
    filled = (jnp.zeros((16, HD), F32) + len_ref[0].astype(F32)).astype(BF16)
    keep_ref[512:528] = filled
    give_ref[512:528] = filled
    for n in range(4):
        copies[n].wait()
        one, two = buf[n, :, 0:HD], buf[n, :, HD : 2 * HD]
        keep_ref[128 * n : 128 * n + 128] = jnp.where(first, one, two)
        give_ref[128 * n : 128 * n + 128] = jnp.where(first, two, one)
    copies[4].wait()
    for k in range(2):
        for b in range(8):
            for r in range(2):
                part = buf[4, 64 * r + 8 * b : 64 * r + 8 * b + 8, HD * k : HD * k + HD]
                for j in range(4):
                    qo_ref[2 * j + k, b, 8 * r : 8 * r + 8] = part


def pair_kernel(pos_ref, keep_ref, got_ref, hw_ref, ow_hbm, kv_ref, ow_ref, full_ref, sem):
    copy = pltpu.make_async_copy(ow_hbm.at[pl.ds(pos_ref[1] * HD, HD)], ow_ref, sem)
    copy.start()
    kv_ref[0, 0:528] = keep_ref[...]
    kv_ref[1, 0:528] = got_ref[...]
    full_ref[...] = jnp.zeros_like(full_ref)
    share = 80 * (pos_ref[0] % 4)
    for m in range(16):
        full_ref[pl.ds(pl.multiple_of(320 * m + share, 16), 80)] = hw_ref[m]
    copy.wait()
    both = jnp.dot(ow_ref[...], full_ref[...], preferred_element_type=F32)
    both = both.T.astype(BF16)
    for k in range(2):
        kv_ref[k, 528:560] = both[32 * k : 32 * k + 32]


def attend_kernel(
    fm_ref,
    pos_ref,
    q_ref,
    kv0_ref,
    kv1_ref,
    kv2_ref,
    kv3_ref,
    prev_ref,
    out_ref,
    pt_ref,
    level_ref,
):
    z, core = pos_ref[0], pos_ref[2] % 2
    planes = (z, z + NZ - 1, z + 1, z + NZ - 2 + 4 * core)
    lane = lax.broadcasted_iota(jnp.int32, (1, HD), 1)
    row_frame = lax.broadcasted_iota(jnp.int32, (128, 1), 0) // 32
    sources = []
    both = jnp.zeros((64, HD), F32)
    for kv_ref, plane in zip((kv0_ref, kv1_ref, kv2_ref, kv3_ref), planes):
        frame = (plane % NZ) // 4
        block_bias = jnp.zeros((128, 1), F32)
        for f in range(FR):
            here = jnp.where(fm_ref[f, frame] == 1, 0.0, NEG)
            block_bias = jnp.where(row_frame == f, here, block_bias)
        block_bias = jnp.broadcast_to(block_bias, (128, 128))
        both = both + jnp.concatenate([kv_ref[0, 528:560], kv_ref[1, 528:560]], 0).astype(F32)
        for k in range(2):
            filled = kv_ref[k, 512:528, :].astype(F32)[0:1]
            cache_bias = jnp.where(lane.astype(F32) < filled, 0.0, NEG)
            sources.append((kv_ref, k, cache_bias, block_bias))
    both = both.astype(BF16)
    part = lax.broadcasted_iota(jnp.int32, (8, 128), 0)

    def block(b, carry):
        q = q_ref[:, b].reshape(128, HD)
        scores = []
        for kv_ref, k, cache_bias, block_bias in sources:
            raw = dot_nt(q, kv_ref[k, 0:256, :]) * C2
            bias = jnp.concatenate(
                [jnp.broadcast_to(cache_bias, (128, 128)), block_bias], axis=1
            )
            scores.append(raw + bias)
        top = functools.reduce(jnp.maximum, scores)
        top = jnp.max(top, axis=1, keepdims=True)
        total = jnp.zeros((128, 256), F32)
        acc = jnp.zeros((128, HD), F32)
        for score, (kv_ref, k, _, _) in zip(scores, sources):
            weights = jnp.exp2(score - top)
            total = total + weights
            acc = acc + jnp.dot(
                weights.astype(BF16), kv_ref[k, 256:512, :], preferred_element_type=F32
            )
        total = jnp.sum(total, axis=1, keepdims=True)
        pt_ref[b] = dot_nt(both, (acc / total).astype(BF16))
        level = jnp.broadcast_to(top + jnp.log2(total), (128, 128)).T[0:8]
        high = level.astype(BF16).astype(F32)
        mid = (level - high).astype(BF16).astype(F32)
        low = level - high - mid
        level_ref[b] = jnp.where(
            part == 0, high, jnp.where(part == 1, mid, jnp.where(part == 2, low, 0.0))
        )
        return carry

    lax.fori_loop(0, 8, block, 0)
    ship(prev_ref, pt_ref, level_ref, out_ref)


def slots(odd, n):
    at = lax.broadcasted_iota(jnp.int32, (128, 128), 0)
    to = lax.broadcasted_iota(jnp.int32, (128, 128), 1)
    free = 5 - 4 * odd
    one = (2 * n + 3 * odd) if n < 2 else (4 - 4 * odd)
    two = (2 * n + 1 + 3 * odd) if n < 2 else 7
    hit = (at % 8 == free) & (to % 8 == one) | (at % 8 == free + 1) & (to % 8 == two)
    return jnp.where((at // 8 == to // 8) & hit, 1.0, 0.0).astype(BF16)


def ship(prev_ref, pt_ref, level_ref, out_ref):
    rims = []
    for side in range(2):
        for f in range(2):
            rims += [prev_ref[f, a, 3 * side : 3 * side + 1, :].astype(F32) for a in range(2)]
    rims = [jnp.concatenate(rims[2 * n : 2 * n + 2], axis=1) for n in range(4)]
    rims = jnp.concatenate(rims + [jnp.zeros((4, 32), F32)], axis=0).astype(BF16)
    column = lax.broadcasted_iota(jnp.int32, (64, 128), 1) % 8
    few = column[0:8]
    item = lax.broadcasted_iota(jnp.int32, (32, 128), 0)
    to = lax.broadcasted_iota(jnp.int32, (32, 128), 1)
    for odd in range(2):
        move = to == 8 * (item // 2) + item % 2 + 5 - 4 * odd
        edge = jnp.dot(rims, jnp.where(move, 1.0, 0.0).astype(BF16), preferred_element_type=F32)
        merged = []
        for b in range(8):
            own, beside = level_ref[b], level_ref[min(max(b - 1 + 2 * odd, 0), 7)]
            merged.append(jnp.where(few == 7 - 7 * odd, beside, own).astype(BF16))
        merged = jnp.concatenate(merged, axis=0)
        tails = [dot_nt(merged, slots(odd, n)) for n in range(3)]
        for b in range(8):
            keep = (column >= 3) if odd else (column <= 4)
            chunk = jnp.where(keep, pt_ref[b], 0.0)
            if 0 <= b - 1 + 2 * odd < 8:
                chunk = jnp.where(column == 7 - 7 * odd, pt_ref[b - 1 + 2 * odd], chunk)
            tail = [t[8 * b : 8 * b + 8] for t in tails] + [edge]
            tail = jnp.concatenate(tail + [jnp.zeros((32, 128), F32)], axis=0)
            out_ref[2 * b + odd] = (chunk + tail).astype(BF16)


def spread_kernel(pos_ref, y_ref, prev_ref, out_ref, rows_ref):
    own = []
    for c in range(2):
        for f in range(2):
            parts = [
                prev_ref[f, a, 2 * c + b : 2 * c + b + 1, :].astype(F32)
                for a in range(2)
                for b in range(2)
            ]
            own.append(jnp.concatenate([jnp.zeros((1, 64), F32)] + parts, axis=1))
    own = jnp.concatenate(own + [jnp.zeros((4, 128), F32)], axis=0).astype(BF16)
    z, h, m = pos_ref[0], pos_ref[1], pos_ref[2]
    odd = z % 2
    to = lax.broadcasted_iota(jnp.int32, (128, 128), 0)
    at = lax.broadcasted_iota(jnp.int32, (128, 128), 1)
    cell = 2 * ((to // 16) % 2) + (to // 4) % 4 + 7 + 4 * odd
    pick = (at // 32 == to % 4) & ((at // 8) % 4 == to // 32) & (at % 8 == cell % 8)
    pick = jnp.where(pick, 1.0, 0.0).astype(BF16)
    to = lax.broadcasted_iota(jnp.int32, (32, 8), 0)
    item = lax.broadcasted_iota(jnp.int32, (32, 8), 1)
    cell_to = 2 * (to // 16) + (to // 4) % 4
    place = (item < 4) & (cell_to == 2 * h + item // 2 + 1) & (to % 4 == item % 2)
    place = jnp.where(place, 1.0, 0.0).astype(BF16)
    earlier = jnp.dot(place, own, preferred_element_type=F32)
    at = lax.broadcasted_iota(jnp.int32, (128, 128), 0)
    to128 = lax.broadcasted_iota(jnp.int32, (128, 128), 1)
    slot = at % 8 - (5 - 4 * odd)
    value = 2 * (at // 8) + slot
    for side in range(2):
        source = jnp.maximum(z - 1, 0) if side == 0 else jnp.minimum(z + 1, NZ - 1)
        there = (z > 0) & (h == 1) if side == 0 else (z < NZ - 1) & (h == 0)
        goal = 64 + 32 * (value // 16) + value % 16 + (16 if side == 0 else 0)
        move = (slot >= 0) & (slot < 2) & (to128 == goal)
        move = jnp.where(move, 1.0, 0.0).astype(BF16)
        rim = jnp.dot(y_ref[source, 16:32], move, preferred_element_type=F32)[8:16]
        rim = jnp.where(there, rim, 0.0).astype(BF16)
        place = (item // 2 == 1 - side) & (item < 4) & (cell_to == 5 * side) & (to % 4 == item % 2)
        place = jnp.where(place, 1.0, 0.0).astype(BF16)
        earlier = earlier + jnp.dot(place, rim, preferred_element_type=F32)
    tails = [[y_ref[n, 0:16], y_ref[n, 16:32]] for n in range(NZ)]
    stacked = jnp.concatenate([t[0] for t in tails], axis=0)
    both = [jnp.where(odd == 1, slots(1, n), slots(0, n)) for n in range(3)]
    first = jnp.dot(stacked, both[0], preferred_element_type=F32)
    second = jnp.dot(stacked, both[1], preferred_element_type=F32)
    stacked = jnp.concatenate([t[1] for t in tails], axis=0)
    third = jnp.dot(stacked, both[2], preferred_element_type=F32)
    for r in range(4):
        levels = []
        for g in range(4):
            n = 16 * (4 * g + r)
            tail = first[n : n + 8] + second[n + 8 : n + 16] + third[n : n + 8]
            levels.append(tail[0:1] + tail[1:2] + tail[2:3])
        top = jnp.maximum(jnp.maximum(levels[0], levels[1]), jnp.maximum(levels[2], levels[3]))
        shares = [jnp.exp2(level - top) for level in levels]
        whole = shares[0] + shares[1] + shares[2] + shares[3]
        value = jnp.zeros((64, 128), F32)
        for g in range(4):
            value = value + (shares[g] / whole) * y_ref[4 * g + r].astype(F32)
        value = jnp.concatenate([value, jnp.zeros((64, 128), F32)], axis=0).astype(BF16)
        moved = dot_nt(pick, value)
        for i in range(4):
            row = 4 * r + i
            rows_ref[row] = moved[32 * i : 32 * i + 32] + jnp.where(m == row, earlier, 0.0)
    below = lax.broadcasted_iota(jnp.int32, (32, 128), 1) % 64 < 32
    for row in range(16):
        under = rows_ref[row + 1] if row < 15 else jnp.zeros((32, 128), F32)
        over = rows_ref[row - 1] if row > 0 else jnp.zeros((32, 128), F32)
        beside = jnp.where(below, under, over).astype(BF16)
        own = rows_ref[row].astype(BF16)
        for k in range(2):
            out_ref[16 * k + row, 0:16] = own[16 * k : 16 * k + 16]
            out_ref[16 * k + row, 16:32] = beside[16 * k : 16 * k + 16]


def decode_kernel(r_ref, w_ref, bias_ref, gain_ref, out_ref, z_ref, taps_ref):
    nothing = jnp.zeros((16, CH), BF16)
    for a in range(2):
        for b in range(2):
            for dt in range(3):
                for k in range(16):
                    i, j, pa, pb = k // 8, k // 4 % 2, k // 2 % 2, k % 2
                    dy, dx = 2 * i + pa + a - 1, 2 * j + pb + b - 1
                    inside = 0 <= dy < 3 and 0 <= dx < 3
                    tap = w_ref[dt, dy, dx] if inside else nothing
                    taps_ref[a, b, dt, 16 * k : 16 * k + 16] = tap
    total = jnp.zeros((32, 128), F32)
    for s in range(32):
        total = total + r_ref[s].astype(F32)
    total = total.astype(BF16).astype(F32)
    z_ref[...] = jnp.zeros_like(z_ref)
    for dr in range(2):
        for cc in range(4):
            at = dr * 16 + cc * 4
            z_ref[dr, cc * 6 + 2 : cc * 6 + 6] = total[at : at + 4, 0:64]
            z_ref[dr, cc * 6 : cc * 6 + 2] = total[at : at + 2, 64:128]
    for a in range(2):
        for b in range(2):
            conv = jnp.zeros((16, CH), F32)
            for dt in range(3):
                pieces = []
                for i in range(2):
                    for j in range(2):
                        start = (b + j) * 6 + dt
                        pieces.append(z_ref[(a + i + 1) % 2, start : start + 16])
                lhs = jnp.concatenate(pieces, axis=1).astype(BF16)
                conv = conv + jnp.dot(lhs, taps_ref[a, b, dt], preferred_element_type=F32)
            conv = conv + bias_ref[...].reshape(1, CH)
            meansq = jnp.mean(conv * conv, axis=1, keepdims=True)
            normed = conv * lax.rsqrt(meansq + 1e-06) * gain_ref[...].reshape(1, CH)
            decoded = (normed / (1.0 + jnp.exp(-normed))).astype(BF16)
            for c in range(2):
                for f in range(FR):
                    out_ref[f, a, 2 * c + b] = decoded[c * 6 + f]


def body(
    queries,
    stretch_keys,
    stretch_values,
    cache_keys,
    cache_values,
    cache_lengths,
    frame_mask,
    out_weight,
    head_weight,
    previous_latent,
    conv_weight,
    conv_bias,
    norm_gain,
):
    z, h, m = lax.axis_index("z"), lax.axis_index("h"), lax.axis_index("mp")
    pos = jnp.stack([z, h, m]).astype(jnp.int32)
    vmem = pl.BlockSpec(memory_space=pltpu.VMEM)
    whole = pl.BlockSpec()
    hbm = pl.BlockSpec(memory_space=pltpu.HBM)
    smem = pl.BlockSpec(memory_space=pltpu.SMEM)

    def call(kernel, name, outs, specs, scratch=(), limit=16, **kw):
        shapes = [jax.ShapeDtypeStruct(shape, kind) for shape, kind in outs]
        return pl.pallas_call(
            kernel,
            out_shape=shapes if len(shapes) > 1 else shapes[0],
            in_specs=specs,
            out_specs=[vmem] * len(shapes) if len(shapes) > 1 else vmem,
            scratch_shapes=scratch,
            compiler_params=pltpu.CompilerParams(vmem_limit_bytes=limit * 1024 * 1024),
            name=name,
            **kw,
        )

    keep, give, q = call(
        pack_kernel,
        "pack",
        (((528, HD), BF16), ((528, HD), BF16), ((8, 8, 16, HD), BF16)),
        [smem] * 2 + [hbm] * 5,
        [pltpu.VMEM((5, 128, 2 * HD), BF16), pltpu.SemaphoreType.DMA((5,))],
        limit=60,
    )(h.reshape(1), cache_lengths, queries, cache_keys, stretch_keys, cache_values, stretch_values)
    got = lax.ppermute(give, "h", [(0, 1), (1, 0)])
    hw = lax.dynamic_slice_in_dim(head_weight, 80 * (z % 4), 80, 0)
    hw = lax.all_to_all(jnp.broadcast_to(hw[None], (16, 80, 64)), "mp", 0, 0, tiled=True)
    q, hw = lax.optimization_barrier((q, hw))
    q = lax.all_to_all(q, ("z", "h"), 0, 0, tiled=True, axis_index_groups=FAR)
    kv = call(
        pair_kernel,
        "pair",
        (((2, 560, HD), BF16),),
        [smem] + [vmem] * 3 + [hbm],
        [pltpu.VMEM((HD, 5120), BF16), pltpu.VMEM((5120, 64), BF16), pltpu.SemaphoreType.DMA],
        limit=32,
        cost_estimate=pl.CostEstimate(flops=10**11, bytes_accessed=10**6, transcendentals=0),
    )(pos, keep, got, hw, out_weight)
    up = lax.ppermute(kv, "z", [(i, (i + 1) % NZ) for i in range(NZ)])
    down = lax.ppermute(kv, "z", [((i + 1) % NZ, i) for i in range(NZ)])
    two = lax.ppermute(
        kv,
        ("z", "mp"),
        [(16 * i + j, 16 * ((i + (2 if j % 2 == 0 else 14)) % NZ) + j) for i in range(NZ) for j in range(16)],
    )
    partial = call(
        attend_kernel,
        "attend",
        (((NZ, 64, 128), BF16),),
        [smem] * 2 + [vmem] * 6,
        [pltpu.VMEM((8, 64, 128), F32), pltpu.VMEM((8, 8, 128), F32)],
        cost_estimate=pl.CostEstimate(flops=10**10, bytes_accessed=10**6, transcendentals=10**6),
    )(frame_mask, pos, q, kv, up, down, two, previous_latent)
    partial = lax.all_to_all(partial, "z", 0, 0, tiled=True)
    spread = call(spread_kernel, "spread", (((32, 32, 128), BF16),), [smem, vmem, whole], [pltpu.VMEM((16, 32, 128), F32)])(
        pos, partial, previous_latent
    )
    spread = lax.all_to_all(spread, ("h", "mp"), 0, 0, tiled=True)
    return call(
        decode_kernel,
        "decode",
        (((FR, 2, 4, CH), BF16),),
        [vmem] + [whole] * 3,
        [pltpu.VMEM((2, 40, 64), F32), pltpu.VMEM((2, 2, 3, 256, CH), BF16)],
    )(spread, conv_weight, conv_bias, norm_gain)


def solution(mesh):
    fine = Mesh(mesh.devices.reshape(NZ, 2, 16), ("z", "h", "mp"))
    seq = ("z", "h")
    return jax.shard_map(
        body,
        mesh=fine,
        in_specs=(
            P(seq, "mp"),
            P(seq, "mp"),
            P(seq, "mp"),
            P(seq, "mp"),
            P(seq, "mp"),
            P(seq),
            P(),
            P("mp", None),
            P("mp", None),
            P(None, "mp", seq, None),
            P(),
            P(),
            P(),
        ),
        out_specs=P(None, "mp", seq, None),
        check_vma=False,
    )
```

```python
import functools
import math

import jax
import jax.numpy as jnp
from jax import lax
from jax.experimental import pallas as pl
from jax.experimental.pallas import tpu as pltpu
from jax.sharding import Mesh, PartitionSpec as P

HD = 128
LATC = 16
CH = 384
FR = 4
NZ = 16
NEG = -1e30
C2 = math.log2(math.e) / math.sqrt(HD)
F32 = jnp.float32
BF16 = jnp.bfloat16
FAR = [[(4 * j + i) * 2 + k for j in range(4) for k in range(2)] for i in range(4)]
NT = (((1,), (1,)), ((), ()))


def dot_nt(a, b):
    return lax.dot_general(a, b, NT, preferred_element_type=F32)


def pack_kernel(
    len_hbm, q_hbm, ck_hbm, sk_hbm, cv_hbm, sv_hbm, keep_ref, give_ref, qo_ref, buf, len_ref, sems
):
    copies = []
    for n, ref in enumerate((ck_hbm, sk_hbm, cv_hbm, sv_hbm, q_hbm)):
        copies.append(pltpu.make_async_copy(ref, buf.at[n], sems.at[n]))
        copies[n].start()
    length = pltpu.make_async_copy(len_hbm, len_ref, sems.at[5])
    length.start()
    first = lax.axis_index("h") == 0
    length.wait()
    filled = (jnp.zeros((16, HD), F32) + len_ref[0].astype(F32)).astype(BF16)
    keep_ref[512:528] = filled
    give_ref[512:528] = filled
    for n in range(4):
        copies[n].wait()
        one, two = buf[n, :, 0:HD], buf[n, :, HD : 2 * HD]
        keep_ref[128 * n : 128 * n + 128] = jnp.where(first, one, two)
        give_ref[128 * n : 128 * n + 128] = jnp.where(first, two, one)
    copies[4].wait()
    for k in range(2):
        for b in range(8):
            for r in range(2):
                part = buf[4, 64 * r + 8 * b : 64 * r + 8 * b + 8, HD * k : HD * k + HD]
                for j in range(4):
                    qo_ref[2 * j + k, b, 8 * r : 8 * r + 8] = part


def pair_kernel(keep_ref, got_ref, hw_ref, ow_hbm, kv_ref, ow_ref, full_ref, sem):
    copy = pltpu.make_async_copy(ow_hbm.at[pl.ds(lax.axis_index("h") * HD, HD)], ow_ref, sem)
    copy.start()
    kv_ref[0, 0:528] = keep_ref[...]
    kv_ref[1, 0:528] = got_ref[...]
    full_ref[...] = jnp.zeros_like(full_ref)
    share = 80 * lax.rem(lax.axis_index("z"), 4)
    for m in range(16):
        full_ref[pl.ds(pl.multiple_of(320 * m + share, 16), 80)] = hw_ref[m]
    copy.wait()
    both = jnp.dot(ow_ref[...], full_ref[...], preferred_element_type=F32)
    both = both.T.astype(BF16)
    for k in range(2):
        for a in range(2):
            at = 32 * a + 16 * k
            kv_ref[k, 528 + 16 * a : 544 + 16 * a] = both[at : at + 16]


def attend_kernel(
    fm_ref,
    q_ref,
    kv0_ref,
    kv1_ref,
    kv2_ref,
    kv3_ref,
    prev_ref,
    out_ref,
    pt_ref,
    level_ref,
):
    z, core = lax.axis_index("z"), lax.rem(lax.axis_index("mp"), 2)
    planes = (z, z + NZ - 1, z + 1, z + NZ - 2 + 4 * core)
    lane = lax.broadcasted_iota(jnp.int32, (1, HD), 1)
    row_frame = lax.broadcasted_iota(jnp.int32, (256, 1), 0) % 128 // 32
    sources = []
    both = jnp.zeros((64, HD), F32)
    for kv_ref, plane in zip((kv0_ref, kv1_ref, kv2_ref, kv3_ref), planes):
        frame = (plane % NZ) // 4
        block_bias = jnp.zeros((256, 1), F32)
        for f in range(FR):
            here = jnp.where(fm_ref[f, frame] == 1, 0.0, NEG)
            block_bias = jnp.where(row_frame == f, here, block_bias)
        block_bias = jnp.broadcast_to(block_bias, (256, 128))
        both = both + jnp.concatenate([kv_ref[0, 528:560], kv_ref[1, 528:560]], 0).astype(F32)
        for k in range(2):
            filled = kv_ref[k, 512:528, :].astype(F32)[0:1]
            cache_bias = jnp.where(lane.astype(F32) < filled, 0.0, NEG)
            sources.append((kv_ref, k, cache_bias, block_bias))
    both = both.astype(BF16)
    part = lax.broadcasted_iota(jnp.int32, (8, 128), 0)

    def block(step, carry):
        q = jnp.concatenate([q_ref[:, 2 * step + i].reshape(128, HD) for i in range(2)], axis=0)
        scores = []
        for kv_ref, k, cache_bias, block_bias in sources:
            raw = dot_nt(q, kv_ref[k, 0:256, :]) * C2
            bias = jnp.concatenate(
                [jnp.broadcast_to(cache_bias, (256, 128)), block_bias], axis=1
            )
            scores.append(raw + bias)
        top = functools.reduce(jnp.maximum, scores)
        top = jnp.max(top, axis=1, keepdims=True)
        total = jnp.zeros((256, 256), F32)
        acc = jnp.zeros((256, HD), F32)
        for score, (kv_ref, k, _, _) in zip(scores, sources):
            weights = jnp.exp2(score - top)
            total = total + weights
            acc = acc + jnp.dot(
                weights.astype(BF16), kv_ref[k, 256:512, :], preferred_element_type=F32
            )
        total = jnp.sum(total, axis=1, keepdims=True)
        attended = (acc / total).astype(BF16)
        level = top + jnp.log2(total)
        for i in range(2):
            b, here = 2 * step + i, slice(128 * i, 128 * i + 128)
            pt_ref[b] = dot_nt(both, attended[here])
            turned = jnp.broadcast_to(level[here], (128, 128)).T[0:8]
            high = turned.astype(BF16).astype(F32)
            mid = (turned - high).astype(BF16).astype(F32)
            low = turned - high - mid
            level_ref[b] = jnp.where(
                part == 0, high, jnp.where(part == 1, mid, jnp.where(part == 2, low, 0.0))
            )
        return carry

    lax.fori_loop(0, 4, block, 0, unroll=4)
    ship(prev_ref, pt_ref, level_ref, out_ref)


def ship(prev_ref, pt_ref, level_ref, out_ref):
    edge = [prev_ref[f, a, 3 * e : 3 * e + 1, :] for e in range(2) for f in range(2) for a in range(2)]
    edge = jnp.concatenate([x.astype(F32) for x in edge], axis=1)
    column = lax.broadcasted_iota(jnp.int32, (32, 128), 1) % 8
    few = column[0:8]
    part = lax.broadcasted_iota(jnp.int32, (8, 128), 0)
    for z in range(NZ):
        b, odd = z // 2, z % 2
        beside = b - 1 + 2 * odd
        low, high = pt_ref[b, 0:32], pt_ref[b, 32:64]
        if odd:
            main = jnp.where(column >= 4, low, pltpu.roll(high, 124, 1))
        else:
            main = jnp.where(column < 4, low, pltpu.roll(high, 4, 1))
        halo = jnp.zeros((8, 128), F32)
        level = level_ref[b]
        for q in range(4):
            if not odd or beside < 8:
                right = pt_ref[beside if odd else b, 8 * q : 8 * q + 8]
                right = pltpu.roll(right, (q if odd else q - 4) % 128, 1)
                halo = jnp.where(few == q, right, halo)
            if odd or beside >= 0:
                left = pt_ref[b if odd else beside, 32 + 8 * q : 40 + 8 * q]
                left = pltpu.roll(left, (q + 1 if odd else q - 3) % 128, 1)
                halo = jnp.where(few == 4 + q, left, halo)
        if 0 <= beside < 8:
            level = jnp.where(few == 7 - 7 * odd, level_ref[beside], level)
        level = jnp.where(part == 3, edge, level)
        out_ref[z] = jnp.concatenate([main, halo, level], axis=0).astype(BF16)


def spread_kernel(y_ref, prev_ref, out_ref, rows_ref):
    z, h, m = (lax.axis_index(axis) for axis in ("z", "h", "mp"))
    odd = lax.rem(z, 2)
    level = []
    for n in range(NZ):
        tail = y_ref[n, 32:48].astype(F32)
        level.append(tail[8:9] + tail[9:10] + tail[10:11])
    level = jnp.concatenate(level, axis=0)
    top = jnp.maximum(
        jnp.maximum(level[0:4], level[4:8]), jnp.maximum(level[8:12], level[12:16])
    )
    share = jnp.exp2(level - jnp.concatenate([top] * 4, axis=0))
    whole = share[0:4] + share[4:8] + share[8:12] + share[12:16]
    share = share / jnp.concatenate([whole] * 4, axis=0)
    column = lax.broadcasted_iota(jnp.int32, (16, 128), 1) % 8
    main_share = jnp.where(odd == 1, pltpu.roll(share, 124, 1), share)
    main_share = jnp.where(column < 4, main_share, pltpu.roll(main_share, 4, 1))
    share = jnp.where(odd == 1, pltpu.roll(share, 4, 1), share)
    halo_share = jnp.zeros((16, 128), F32)
    for q in range(4):
        halo_share = jnp.where(column == q, pltpu.roll(share, (q - 4) % 128, 1), halo_share)
        halo_share = jnp.where(column == 4 + q, pltpu.roll(share, (q - 3) % 128, 1), halo_share)
    to = lax.broadcasted_iota(jnp.int32, (128, 128), 0)
    at = lax.broadcasted_iota(jnp.int32, (128, 128), 1)
    same = (at // 32 == to % 4) & ((at // 8) % 4 == to // 32)
    goal = 2 * ((to // 16) % 2) + (to // 4) % 4 - 1
    own = same & (goal >= 0) & (goal < 4)
    pick = [
        own & (at % 8 == goal + 4 * odd),
        own & (at % 8 == goal + 4 - 4 * odd),
        same & ((goal == 4) & (at % 8 < 4) | (goal == -1) & (at % 8 >= 4)),
    ]
    pick = jnp.concatenate([jnp.where(x, 1.0, 0.0).astype(BF16) for x in pick], axis=1)
    lane = lax.broadcasted_iota(jnp.int32, (1, 128), 1)
    earlier = []
    for c in range(2):
        for f in range(2):
            parts = [
                prev_ref[f, a, 2 * c + b : 2 * c + b + 1, :].astype(F32)
                for b in range(2)
                for a in range(2)
            ]
            earlier.append(jnp.concatenate([jnp.zeros((1, 64), F32)] + parts, axis=1))
    rim = y_ref[jnp.maximum(z - 1, 0), 32:48].astype(F32)[11:12]
    rim = jnp.where((z > 0) & (h == 1), rim, 0.0)
    for f in range(2):
        earlier.append(jnp.where(lane >= 96, pltpu.roll(rim, 32 - 32 * f, 1), 0.0))
    rim = y_ref[jnp.minimum(z + 1, NZ - 1), 32:48].astype(F32)[11:12]
    rim = jnp.where((z < NZ - 1) & (h == 0), rim, 0.0)
    for f in range(2):
        earlier.append(
            jnp.where((lane >= 64) & (lane < 96), pltpu.roll(rim, 64 - 32 * f, 1), 0.0)
        )
    to = lax.broadcasted_iota(jnp.int32, (32, 8), 0)
    item = lax.broadcasted_iota(jnp.int32, (32, 8), 1)
    cell = 2 * (to // 16) + (to // 4) % 4
    place = (item < 4) & (cell == 2 * h + item // 2 + 1)
    place = place | (item // 2 == 2) & (cell == 0) | (item // 2 == 3) & (cell == 5)
    place = jnp.where(place & (to % 4 == item % 2), 1.0, 0.0).astype(BF16)
    earlier = jnp.dot(
        place, jnp.concatenate(earlier, axis=0).astype(BF16), preferred_element_type=F32
    )
    few = column[0:8]
    blank = jnp.zeros((32, 128), F32)
    for r in range(4):
        main = jnp.zeros((32, 128), F32)
        halo = jnp.zeros((8, 128), F32)
        for g in range(4):
            n = 4 * g + r
            main = main + main_share[n : n + 1] * y_ref[n, 0:32].astype(F32)
            halo = halo + halo_share[n : n + 1] * y_ref[n, 32:48].astype(F32)[0:8]
        right = jnp.concatenate([jnp.where(few == q, halo, 0.0) for q in range(4)], axis=0)
        left = jnp.concatenate([jnp.where(few == 4 + q, halo, 0.0) for q in range(4)], axis=0)
        value = jnp.concatenate(
            [
                jnp.concatenate([main, blank, right], axis=1),
                jnp.concatenate([blank, main, left], axis=1),
                jnp.zeros((64, 384), F32),
            ],
            axis=0,
        )
        moved = dot_nt(pick, value.astype(BF16))
        for i in range(4):
            row = 4 * r + i
            rows_ref[row] = moved[32 * i : 32 * i + 32] + jnp.where(m == row, earlier, 0.0)
    below = lax.broadcasted_iota(jnp.int32, (32, 128), 1) % 32 < 16
    for row in range(16):
        under = rows_ref[row + 1] if row < 15 else jnp.zeros((32, 128), F32)
        over = rows_ref[row - 1] if row > 0 else jnp.zeros((32, 128), F32)
        beside = jnp.where(below, under, over).astype(BF16)
        own = rows_ref[row].astype(BF16)
        for k in range(2):
            out_ref[16 * k + row, 0:16] = own[16 * k : 16 * k + 16]
            out_ref[16 * k + row, 16:32] = beside[16 * k : 16 * k + 16]


def decode_kernel(r_ref, w_ref, bias_ref, gain_ref, out_ref, z_ref, taps_ref):
    nothing = jnp.zeros((16, CH), BF16)
    for a in range(2):
        for b in range(2):
            for dt in range(3):
                for k in range(16):
                    i, j, pb, pa = k // 8, k // 4 % 2, k // 2 % 2, k % 2
                    dy, dx = 2 * i + pa + a - 1, 2 * j + pb + b - 1
                    inside = 0 <= dy < 3 and 0 <= dx < 3
                    tap = w_ref[dt, dy, dx] if inside else nothing
                    taps_ref[a, b, dt, 16 * k : 16 * k + 16] = tap
    total = jnp.zeros((32, 128), F32)
    for s in range(32):
        total = total + r_ref[s].astype(F32)
    total = total.astype(BF16).astype(F32)
    z_ref[...] = jnp.zeros_like(z_ref)
    for dr in range(2):
        for cc in range(4):
            at = dr * 16 + cc * 4
            z_ref[dr, cc * 6 + 2 : cc * 6 + 6] = total[at : at + 4, 0:64]
            z_ref[dr, cc * 6 : cc * 6 + 2] = total[at : at + 2, 64:128]
    for a in range(2):
        for b in range(2):
            conv = jnp.zeros((16, CH), F32)
            for dt in range(3):
                pieces = []
                for i in range(2):
                    for j in range(2):
                        start = (b + j) * 6 + dt
                        pieces.append(z_ref[(a + i + 1) % 2, start : start + 16])
                lhs = jnp.concatenate(pieces, axis=1).astype(BF16)
                conv = conv + jnp.dot(lhs, taps_ref[a, b, dt], preferred_element_type=F32)
            conv = conv + bias_ref[...].reshape(1, CH)
            meansq = jnp.mean(conv * conv, axis=1, keepdims=True)
            normed = conv * lax.rsqrt(meansq + 1e-06) * gain_ref[...].reshape(1, CH)
            decoded = (normed / (1.0 + jnp.exp(-normed))).astype(BF16)
            for c in range(2):
                for f in range(FR):
                    out_ref[f, a, 2 * c + b] = decoded[c * 6 + f]


def body(
    queries,
    stretch_keys,
    stretch_values,
    cache_keys,
    cache_values,
    cache_lengths,
    frame_mask,
    out_weight,
    head_weight,
    previous_latent,
    conv_weight,
    conv_bias,
    norm_gain,
):
    z = lax.axis_index("z")
    vmem = pl.BlockSpec(memory_space=pltpu.VMEM)
    whole = pl.BlockSpec()
    hbm = pl.BlockSpec(memory_space=pltpu.HBM)
    smem = pl.BlockSpec(memory_space=pltpu.SMEM)

    def call(kernel, name, outs, specs, scratch=(), limit=16, **kw):
        shapes = [jax.ShapeDtypeStruct(shape, kind) for shape, kind in outs]
        return pl.pallas_call(
            kernel,
            out_shape=shapes if len(shapes) > 1 else shapes[0],
            in_specs=specs,
            out_specs=[vmem] * len(shapes) if len(shapes) > 1 else vmem,
            scratch_shapes=scratch,
            compiler_params=pltpu.CompilerParams(vmem_limit_bytes=limit * 1024 * 1024),
            name=name,
            **kw,
        )

    keep, give, q = call(
        pack_kernel,
        "pack",
        (((528, HD), BF16), ((528, HD), BF16), ((8, 8, 16, HD), BF16)),
        [hbm] * 6,
        [
            pltpu.VMEM((5, 128, 2 * HD), BF16),
            pltpu.SMEM((1,), jnp.int32),
            pltpu.SemaphoreType.DMA((6,)),
        ],
        limit=60,
    )(cache_lengths, queries, cache_keys, stretch_keys, cache_values, stretch_values)
    got = lax.ppermute(give, "h", [(0, 1), (1, 0)])
    hw = lax.dynamic_slice_in_dim(head_weight, 80 * (z % 4), 80, 0)
    hw = lax.all_to_all(jnp.broadcast_to(hw[None], (16, 80, 64)), "mp", 0, 0, tiled=True)
    q, hw = lax.optimization_barrier((q, hw))
    q = lax.all_to_all(q, ("z", "h"), 0, 0, tiled=True, axis_index_groups=FAR)
    kv = call(
        pair_kernel,
        "pair",
        (((2, 560, HD), BF16),),
        [vmem] * 3 + [hbm],
        [pltpu.VMEM((HD, 5120), BF16), pltpu.VMEM((5120, 64), BF16), pltpu.SemaphoreType.DMA],
        limit=52,
        cost_estimate=pl.CostEstimate(flops=10**11, bytes_accessed=10**6, transcendentals=0),
    )(keep, got, hw, out_weight)
    up = lax.ppermute(kv, "z", [(i, (i + 1) % NZ) for i in range(NZ)])
    down = lax.ppermute(kv, "z", [((i + 1) % NZ, i) for i in range(NZ)])
    two = lax.ppermute(
        kv,
        ("z", "mp"),
        [(16 * i + j, 16 * ((i + (2 if j % 2 == 0 else 14)) % NZ) + j) for i in range(NZ) for j in range(16)],
    )
    partial = call(
        attend_kernel,
        "attend",
        (((NZ, 48, 128), BF16),),
        [smem] + [vmem] * 6,
        [pltpu.VMEM((8, 64, 128), F32), pltpu.VMEM((8, 8, 128), F32)],
        cost_estimate=pl.CostEstimate(flops=10**10, bytes_accessed=10**6, transcendentals=10**6),
    )(frame_mask, q, kv, up, down, two, previous_latent)
    partial = lax.all_to_all(partial, "z", 0, 0, tiled=True)
    spread = call(spread_kernel, "spread", (((32, 32, 128), BF16),), [vmem, whole], [pltpu.VMEM((16, 32, 128), F32)])(
        partial, previous_latent
    )
    spread = lax.all_to_all(spread, ("h", "mp"), 0, 0, tiled=True)
    return call(
        decode_kernel,
        "decode",
        (((FR, 2, 4, CH), BF16),),
        [vmem] + [whole] * 3,
        [pltpu.VMEM((2, 40, 64), F32), pltpu.VMEM((2, 2, 3, 256, CH), BF16)],
    )(spread, conv_weight, conv_bias, norm_gain)


def solution(mesh):
    fine = Mesh(mesh.devices.reshape(NZ, 2, 16), ("z", "h", "mp"))
    seq = ("z", "h")
    return jax.shard_map(
        body,
        mesh=fine,
        in_specs=(
            P(seq, "mp"),
            P(seq, "mp"),
            P(seq, "mp"),
            P(seq, "mp"),
            P(seq, "mp"),
            P(seq),
            P(),
            P("mp", None),
            P("mp", None),
            P(None, "mp", seq, None),
            P(),
            P(),
            P(),
        ),
        out_specs=P(None, "mp", seq, None),
        check_vma=False,
    )
```

```python
import functools
import math

import jax
import jax.numpy as jnp
from jax import lax
from jax.experimental import pallas as pl
from jax.experimental.pallas import tpu as pltpu
from jax.sharding import Mesh, PartitionSpec as P

HD = 128
LATC = 16
CH = 384
FR = 4
NZ = 16
NEG = -1e30
C2 = math.log2(math.e) / math.sqrt(HD)
F32 = jnp.float32
BF16 = jnp.bfloat16
FAR = [[(4 * j + i) * 2 + k for j in range(4) for k in range(2)] for i in range(4)]
NT = (((1,), (1,)), ((), ()))


def dot_nt(a, b):
    return lax.dot_general(a, b, NT, preferred_element_type=F32)


def pack_kernel(
    len_hbm, q_hbm, ck_hbm, sk_hbm, cv_hbm, sv_hbm, keep_ref, give_ref, qo_ref, buf, len_ref, sems
):
    copies = []
    for n, ref in enumerate((ck_hbm, sk_hbm, cv_hbm, sv_hbm, q_hbm)):
        copies.append(pltpu.make_async_copy(ref, buf.at[n], sems.at[n]))
        copies[n].start()
    length = pltpu.make_async_copy(len_hbm, len_ref, sems.at[5])
    length.start()
    first = lax.axis_index("h") == 0
    length.wait()
    filled = (jnp.zeros((16, HD), F32) + len_ref[0].astype(F32)).astype(BF16)
    keep_ref[512:528] = filled
    give_ref[512:528] = filled
    for n in range(4):
        copies[n].wait()
        one, two = buf[n, :, 0:HD], buf[n, :, HD : 2 * HD]
        keep_ref[128 * n : 128 * n + 128] = jnp.where(first, one, two)
        give_ref[128 * n : 128 * n + 128] = jnp.where(first, two, one)
    copies[4].wait()
    for k in range(2):
        for b in range(8):
            for r in range(2):
                part = buf[4, 64 * r + 8 * b : 64 * r + 8 * b + 8, HD * k : HD * k + HD]
                for j in range(4):
                    qo_ref[2 * j + k, b, 8 * r : 8 * r + 8] = part


def pair_kernel(keep_ref, got_ref, hw_ref, ow_hbm, kv_ref, ow_ref, full_ref, sem):
    copy = pltpu.make_async_copy(ow_hbm.at[pl.ds(lax.axis_index("h") * HD, HD)], ow_ref, sem)
    copy.start()
    kv_ref[0, 0:528] = keep_ref[...]
    kv_ref[1, 0:528] = got_ref[...]
    full_ref[...] = jnp.zeros_like(full_ref)
    share = 80 * lax.rem(lax.axis_index("z"), 4)
    for m in range(16):
        full_ref[pl.ds(pl.multiple_of(320 * m + share, 16), 80)] = hw_ref[m]
    copy.wait()
    both = jnp.dot(ow_ref[...], full_ref[...], preferred_element_type=F32)
    both = both.T.astype(BF16)
    for k in range(2):
        for a in range(2):
            at = 32 * a + 16 * k
            kv_ref[k, 528 + 16 * a : 544 + 16 * a] = both[at : at + 16]


def attend(fm_ref, q_ref, planes, emit):
    lane = lax.broadcasted_iota(jnp.int32, (1, HD), 1)
    row_frame = lax.broadcasted_iota(jnp.int32, (256, 1), 0) % 128 // 32
    sources = []
    for kv_ref, plane in planes:
        frame = (plane % NZ) // 4
        block_bias = jnp.zeros((256, 1), F32)
        for f in range(FR):
            here = jnp.where(fm_ref[f, frame] == 1, 0.0, NEG)
            block_bias = jnp.where(row_frame == f, here, block_bias)
        block_bias = jnp.broadcast_to(block_bias, (256, 128))
        for k in range(2):
            filled = kv_ref[k, 512:528, :].astype(F32)[0:1]
            cache_bias = jnp.where(lane.astype(F32) < filled, 0.0, NEG)
            sources.append((kv_ref, k, cache_bias, block_bias))

    def block(step, carry):
        q = jnp.concatenate([q_ref[:, 2 * step + i].reshape(128, HD) for i in range(2)], axis=0)
        scores = []
        for kv_ref, k, cache_bias, block_bias in sources:
            raw = dot_nt(q, kv_ref[k, 0:256, :]) * C2
            bias = jnp.concatenate(
                [jnp.broadcast_to(cache_bias, (256, 128)), block_bias], axis=1
            )
            scores.append(raw + bias)
        top = functools.reduce(jnp.maximum, scores)
        top = jnp.max(top, axis=1, keepdims=True)
        total = jnp.zeros((256, 256), F32)
        acc = jnp.zeros((256, HD), F32)
        for score, (kv_ref, k, _, _) in zip(scores, sources):
            weights = jnp.exp2(score - top)
            total = total + weights
            acc = acc + jnp.dot(
                weights.astype(BF16), kv_ref[k, 256:512, :], preferred_element_type=F32
            )
        total = jnp.sum(total, axis=1, keepdims=True)
        attended = (acc / total).astype(BF16)
        level = top + jnp.log2(total)
        for i in range(2):
            here = slice(128 * i, 128 * i + 128)
            turned = jnp.broadcast_to(level[here], (128, 128)).T[0:8]
            emit(2 * step + i, attended[here], turned)
        return carry

    lax.fori_loop(0, 4, block, 0, unroll=4)


def shares(*refs):
    return sum(jnp.concatenate([ref[0, 528:560], ref[1, 528:560]], 0).astype(F32) for ref in refs)


def first_kernel(fm_ref, q_ref, kv0_ref, kv3_ref, out_ref, level_ref, both_ref):
    z, core = lax.axis_index("z"), lax.rem(lax.axis_index("mp"), 2)

    def emit(b, attended, level):
        out_ref[b] = attended
        level_ref[b] = level

    attend(fm_ref, q_ref, ((kv0_ref, z), (kv3_ref, z + NZ - 2 + 4 * core)), emit)
    both_ref[...] = shares(kv0_ref, kv3_ref)


def second_kernel(
    fm_ref,
    q_ref,
    kv1_ref,
    kv2_ref,
    first_ref,
    first_level_ref,
    first_both_ref,
    prev_ref,
    out_ref,
    pt_ref,
    level_ref,
):
    z = lax.axis_index("z")
    both = (first_both_ref[...] + shares(kv1_ref, kv2_ref)).astype(BF16)
    part = lax.broadcasted_iota(jnp.int32, (8, 128), 0)

    def emit(b, attended, level):
        other = first_level_ref[b]
        top = jnp.maximum(level, other)
        share, other = jnp.exp2(level - top), jnp.exp2(other - top)
        whole = share + other
        here, there = dot_nt(both, attended), dot_nt(both, first_ref[b])
        pt_ref[b] = (share / whole)[0:1] * here + (other / whole)[0:1] * there
        level = top + jnp.log2(whole)
        high = level.astype(BF16).astype(F32)
        mid = (level - high).astype(BF16).astype(F32)
        low = level - high - mid
        level_ref[b] = jnp.where(
            part == 0, high, jnp.where(part == 1, mid, jnp.where(part == 2, low, 0.0))
        )

    attend(fm_ref, q_ref, ((kv1_ref, z + NZ - 1), (kv2_ref, z + 1)), emit)
    ship(prev_ref, pt_ref, level_ref, out_ref)


def ship(prev_ref, pt_ref, level_ref, out_ref):
    edge = [prev_ref[f, a, 3 * e : 3 * e + 1, :] for e in range(2) for f in range(2) for a in range(2)]
    edge = jnp.concatenate([x.astype(F32) for x in edge], axis=1)
    column = lax.broadcasted_iota(jnp.int32, (32, 128), 1) % 8
    few = column[0:8]
    part = lax.broadcasted_iota(jnp.int32, (8, 128), 0)
    for z in range(NZ):
        b, odd = z // 2, z % 2
        beside = b - 1 + 2 * odd
        low, high = pt_ref[b, 0:32], pt_ref[b, 32:64]
        if odd:
            main = jnp.where(column >= 4, low, pltpu.roll(high, 124, 1))
        else:
            main = jnp.where(column < 4, low, pltpu.roll(high, 4, 1))
        halo = jnp.zeros((8, 128), F32)
        level = level_ref[b]
        for q in range(4):
            if not odd or beside < 8:
                right = pt_ref[beside if odd else b, 8 * q : 8 * q + 8]
                right = pltpu.roll(right, (q if odd else q - 4) % 128, 1)
                halo = jnp.where(few == q, right, halo)
            if odd or beside >= 0:
                left = pt_ref[b if odd else beside, 32 + 8 * q : 40 + 8 * q]
                left = pltpu.roll(left, (q + 1 if odd else q - 3) % 128, 1)
                halo = jnp.where(few == 4 + q, left, halo)
        if 0 <= beside < 8:
            level = jnp.where(few == 7 - 7 * odd, level_ref[beside], level)
        level = jnp.where(part == 3, edge, level)
        out_ref[z] = jnp.concatenate([main, halo, level], axis=0).astype(BF16)


def spread_kernel(y_ref, prev_ref, out_ref, rows_ref):
    z, h, m = (lax.axis_index(axis) for axis in ("z", "h", "mp"))
    odd = lax.rem(z, 2)
    level = []
    for n in range(NZ):
        tail = y_ref[n, 32:48].astype(F32)
        level.append(tail[8:9] + tail[9:10] + tail[10:11])
    level = jnp.concatenate(level, axis=0)
    top = jnp.maximum(
        jnp.maximum(level[0:4], level[4:8]), jnp.maximum(level[8:12], level[12:16])
    )
    share = jnp.exp2(level - jnp.concatenate([top] * 4, axis=0))
    whole = share[0:4] + share[4:8] + share[8:12] + share[12:16]
    share = share / jnp.concatenate([whole] * 4, axis=0)
    column = lax.broadcasted_iota(jnp.int32, (16, 128), 1) % 8
    main_share = jnp.where(odd == 1, pltpu.roll(share, 124, 1), share)
    main_share = jnp.where(column < 4, main_share, pltpu.roll(main_share, 4, 1))
    share = jnp.where(odd == 1, pltpu.roll(share, 4, 1), share)
    halo_share = jnp.zeros((16, 128), F32)
    for q in range(4):
        halo_share = jnp.where(column == q, pltpu.roll(share, (q - 4) % 128, 1), halo_share)
        halo_share = jnp.where(column == 4 + q, pltpu.roll(share, (q - 3) % 128, 1), halo_share)
    to = lax.broadcasted_iota(jnp.int32, (128, 128), 0)
    at = lax.broadcasted_iota(jnp.int32, (128, 128), 1)
    same = (at // 32 == to % 4) & ((at // 8) % 4 == to // 32)
    goal = 2 * ((to // 16) % 2) + (to // 4) % 4 - 1
    own = same & (goal >= 0) & (goal < 4)
    pick = [
        own & (at % 8 == goal + 4 * odd),
        own & (at % 8 == goal + 4 - 4 * odd),
        same & ((goal == 4) & (at % 8 < 4) | (goal == -1) & (at % 8 >= 4)),
    ]
    pick = jnp.concatenate([jnp.where(x, 1.0, 0.0).astype(BF16) for x in pick], axis=1)
    lane = lax.broadcasted_iota(jnp.int32, (1, 128), 1)
    earlier = []
    for c in range(2):
        for f in range(2):
            parts = [
                prev_ref[f, a, 2 * c + b : 2 * c + b + 1, :].astype(F32)
                for b in range(2)
                for a in range(2)
            ]
            earlier.append(jnp.concatenate([jnp.zeros((1, 64), F32)] + parts, axis=1))
    rim = y_ref[jnp.maximum(z - 1, 0), 32:48].astype(F32)[11:12]
    rim = jnp.where((z > 0) & (h == 1), rim, 0.0)
    for f in range(2):
        earlier.append(jnp.where(lane >= 96, pltpu.roll(rim, 32 - 32 * f, 1), 0.0))
    rim = y_ref[jnp.minimum(z + 1, NZ - 1), 32:48].astype(F32)[11:12]
    rim = jnp.where((z < NZ - 1) & (h == 0), rim, 0.0)
    for f in range(2):
        earlier.append(
            jnp.where((lane >= 64) & (lane < 96), pltpu.roll(rim, 64 - 32 * f, 1), 0.0)
        )
    to = lax.broadcasted_iota(jnp.int32, (32, 8), 0)
    item = lax.broadcasted_iota(jnp.int32, (32, 8), 1)
    cell = 2 * (to // 16) + (to // 4) % 4
    place = (item < 4) & (cell == 2 * h + item // 2 + 1)
    place = place | (item // 2 == 2) & (cell == 0) | (item // 2 == 3) & (cell == 5)
    place = jnp.where(place & (to % 4 == item % 2), 1.0, 0.0).astype(BF16)
    earlier = jnp.dot(
        place, jnp.concatenate(earlier, axis=0).astype(BF16), preferred_element_type=F32
    )
    few = column[0:8]
    blank = jnp.zeros((32, 128), F32)
    for r in range(4):
        main = jnp.zeros((32, 128), F32)
        halo = jnp.zeros((8, 128), F32)
        for g in range(4):
            n = 4 * g + r
            main = main + main_share[n : n + 1] * y_ref[n, 0:32].astype(F32)
            halo = halo + halo_share[n : n + 1] * y_ref[n, 32:48].astype(F32)[0:8]
        right = jnp.concatenate([jnp.where(few == q, halo, 0.0) for q in range(4)], axis=0)
        left = jnp.concatenate([jnp.where(few == 4 + q, halo, 0.0) for q in range(4)], axis=0)
        value = jnp.concatenate(
            [
                jnp.concatenate([main, blank, right], axis=1),
                jnp.concatenate([blank, main, left], axis=1),
                jnp.zeros((64, 384), F32),
            ],
            axis=0,
        )
        moved = dot_nt(pick, value.astype(BF16))
        for i in range(4):
            row = 4 * r + i
            rows_ref[row] = moved[32 * i : 32 * i + 32] + jnp.where(m == row, earlier, 0.0)
    below = lax.broadcasted_iota(jnp.int32, (32, 128), 1) % 32 < 16
    for row in range(16):
        under = rows_ref[row + 1] if row < 15 else jnp.zeros((32, 128), F32)
        over = rows_ref[row - 1] if row > 0 else jnp.zeros((32, 128), F32)
        beside = jnp.where(below, under, over).astype(BF16)
        own = rows_ref[row].astype(BF16)
        for k in range(2):
            out_ref[16 * k + row, 0:16] = own[16 * k : 16 * k + 16]
            out_ref[16 * k + row, 16:32] = beside[16 * k : 16 * k + 16]


def decode_kernel(r_ref, w_ref, bias_ref, gain_ref, out_ref, z_ref, taps_ref):
    nothing = jnp.zeros((16, CH), BF16)
    for a in range(2):
        for b in range(2):
            for dt in range(3):
                for k in range(16):
                    i, j, pb, pa = k // 8, k // 4 % 2, k // 2 % 2, k % 2
                    dy, dx = 2 * i + pa + a - 1, 2 * j + pb + b - 1
                    inside = 0 <= dy < 3 and 0 <= dx < 3
                    tap = w_ref[dt, dy, dx] if inside else nothing
                    taps_ref[a, b, dt, 16 * k : 16 * k + 16] = tap
    total = jnp.zeros((32, 128), F32)
    for s in range(32):
        total = total + r_ref[s].astype(F32)
    total = total.astype(BF16).astype(F32)
    z_ref[...] = jnp.zeros_like(z_ref)
    for dr in range(2):
        for cc in range(4):
            at = dr * 16 + cc * 4
            z_ref[dr, cc * 6 + 2 : cc * 6 + 6] = total[at : at + 4, 0:64]
            z_ref[dr, cc * 6 : cc * 6 + 2] = total[at : at + 2, 64:128]
    for a in range(2):
        for b in range(2):
            conv = jnp.zeros((16, CH), F32)
            for dt in range(3):
                pieces = []
                for i in range(2):
                    for j in range(2):
                        start = (b + j) * 6 + dt
                        pieces.append(z_ref[(a + i + 1) % 2, start : start + 16])
                lhs = jnp.concatenate(pieces, axis=1).astype(BF16)
                conv = conv + jnp.dot(lhs, taps_ref[a, b, dt], preferred_element_type=F32)
            conv = conv + bias_ref[...].reshape(1, CH)
            meansq = jnp.mean(conv * conv, axis=1, keepdims=True)
            normed = conv * lax.rsqrt(meansq + 1e-06) * gain_ref[...].reshape(1, CH)
            decoded = (normed / (1.0 + jnp.exp(-normed))).astype(BF16)
            for c in range(2):
                for f in range(FR):
                    out_ref[f, a, 2 * c + b] = decoded[c * 6 + f]


def body(
    queries,
    stretch_keys,
    stretch_values,
    cache_keys,
    cache_values,
    cache_lengths,
    frame_mask,
    out_weight,
    head_weight,
    previous_latent,
    conv_weight,
    conv_bias,
    norm_gain,
):
    z = lax.axis_index("z")
    vmem = pl.BlockSpec(memory_space=pltpu.VMEM)
    whole = pl.BlockSpec()
    hbm = pl.BlockSpec(memory_space=pltpu.HBM)
    smem = pl.BlockSpec(memory_space=pltpu.SMEM)

    def call(kernel, name, outs, specs, scratch=(), limit=16, **kw):
        shapes = [jax.ShapeDtypeStruct(shape, kind) for shape, kind in outs]
        return pl.pallas_call(
            kernel,
            out_shape=shapes if len(shapes) > 1 else shapes[0],
            in_specs=specs,
            out_specs=[vmem] * len(shapes) if len(shapes) > 1 else vmem,
            scratch_shapes=scratch,
            compiler_params=pltpu.CompilerParams(vmem_limit_bytes=limit * 1024 * 1024),
            name=name,
            **kw,
        )

    keep, give, q = call(
        pack_kernel,
        "pack",
        (((528, HD), BF16), ((528, HD), BF16), ((8, 8, 16, HD), BF16)),
        [hbm] * 6,
        [
            pltpu.VMEM((5, 128, 2 * HD), BF16),
            pltpu.SMEM((1,), jnp.int32),
            pltpu.SemaphoreType.DMA((6,)),
        ],
        limit=60,
    )(cache_lengths, queries, cache_keys, stretch_keys, cache_values, stretch_values)
    got = lax.ppermute(give, "h", [(0, 1), (1, 0)])
    hw = lax.dynamic_slice_in_dim(head_weight, 80 * (z % 4), 80, 0)
    hw = lax.all_to_all(jnp.broadcast_to(hw[None], (16, 80, 64)), "mp", 0, 0, tiled=True)
    q, hw = lax.optimization_barrier((q, hw))
    q = lax.all_to_all(q, ("z", "h"), 0, 0, tiled=True, axis_index_groups=FAR)
    kv = call(
        pair_kernel,
        "pair",
        (((2, 560, HD), BF16),),
        [vmem] * 3 + [hbm],
        [pltpu.VMEM((HD, 5120), BF16), pltpu.VMEM((5120, 64), BF16), pltpu.SemaphoreType.DMA],
        limit=52,
        cost_estimate=pl.CostEstimate(flops=10**11, bytes_accessed=10**6, transcendentals=0),
    )(keep, got, hw, out_weight)
    up = lax.ppermute(kv, "z", [(i, (i + 1) % NZ) for i in range(NZ)])
    down = lax.ppermute(kv, "z", [((i + 1) % NZ, i) for i in range(NZ)])
    two = lax.ppermute(
        kv,
        ("z", "mp"),
        [(16 * i + j, 16 * ((i + (2 if j % 2 == 0 else 14)) % NZ) + j) for i in range(NZ) for j in range(16)],
    )
    cost = pl.CostEstimate(flops=10**10, bytes_accessed=10**6, transcendentals=10**6)
    first = call(
        first_kernel,
        "first",
        (((8, 128, HD), BF16), ((8, 8, 128), F32), ((64, HD), F32)),
        [smem] + [vmem] * 3,
        cost_estimate=cost,
    )(frame_mask, q, kv, two)
    partial = call(
        second_kernel,
        "second",
        (((NZ, 48, 128), BF16),),
        [smem] + [vmem] * 7,
        [pltpu.VMEM((8, 64, 128), F32), pltpu.VMEM((8, 8, 128), F32)],
        cost_estimate=cost,
    )(frame_mask, q, up, down, *first, previous_latent)
    partial = lax.all_to_all(partial, "z", 0, 0, tiled=True)
    spread = call(spread_kernel, "spread", (((32, 32, 128), BF16),), [vmem, whole], [pltpu.VMEM((16, 32, 128), F32)])(
        partial, previous_latent
    )
    spread = lax.all_to_all(spread, ("h", "mp"), 0, 0, tiled=True)
    return call(
        decode_kernel,
        "decode",
        (((FR, 2, 4, CH), BF16),),
        [vmem] + [whole] * 3,
        [pltpu.VMEM((2, 40, 64), F32), pltpu.VMEM((2, 2, 3, 256, CH), BF16)],
    )(spread, conv_weight, conv_bias, norm_gain)


def solution(mesh):
    fine = Mesh(mesh.devices.reshape(NZ, 2, 16), ("z", "h", "mp"))
    seq = ("z", "h")
    return jax.shard_map(
        body,
        mesh=fine,
        in_specs=(
            P(seq, "mp"),
            P(seq, "mp"),
            P(seq, "mp"),
            P(seq, "mp"),
            P(seq, "mp"),
            P(seq),
            P(),
            P("mp", None),
            P("mp", None),
            P(None, "mp", seq, None),
            P(),
            P(),
            P(),
        ),
        out_specs=P(None, "mp", seq, None),
        check_vma=False,
    )
```

```python
import functools
import math

import jax
import jax.numpy as jnp
from jax import lax
from jax.experimental import pallas as pl
from jax.experimental.pallas import tpu as pltpu
from jax.sharding import Mesh, PartitionSpec as P

HD = 128
LATC = 16
CH = 384
FR = 4
NZ = 16
NEG = -1e30
C2 = math.log2(math.e) / math.sqrt(HD)
F32 = jnp.float32
BF16 = jnp.bfloat16
FAR = [[(4 * j + i) * 2 + k for j in range(4) for k in range(2)] for i in range(4)]
NT = (((1,), (1,)), ((), ()))


def dot_nt(a, b):
    return lax.dot_general(a, b, NT, preferred_element_type=F32)


def pack_kernel(
    len_hbm, q_hbm, ck_hbm, sk_hbm, cv_hbm, sv_hbm, keep_ref, give_ref, raw_ref, qo_ref, buf, len_ref, sems
):
    copies = []
    for n, ref in enumerate((ck_hbm, sk_hbm, cv_hbm, sv_hbm, q_hbm)):
        copies.append(pltpu.make_async_copy(ref, buf.at[n], sems.at[n]))
        copies[n].start()
    length = pltpu.make_async_copy(len_hbm, len_ref, sems.at[5])
    length.start()
    first = lax.axis_index("h") == 0
    length.wait()
    filled = (jnp.zeros((16, HD), F32) + len_ref[0].astype(F32)).astype(BF16)
    keep_ref[512:528] = filled
    give_ref[512:528] = filled
    raw_ref[512:528] = jnp.concatenate([filled, filled], axis=1)
    for n in range(4):
        copies[n].wait()
        raw_ref[128 * n : 128 * n + 128] = buf[n]
        one, two = buf[n, :, 0:HD], buf[n, :, HD : 2 * HD]
        keep_ref[128 * n : 128 * n + 128] = jnp.where(first, one, two)
        give_ref[128 * n : 128 * n + 128] = jnp.where(first, two, one)
    copies[4].wait()
    for k in range(2):
        for b in range(8):
            for r in range(2):
                part = buf[4, 64 * r + 8 * b : 64 * r + 8 * b + 8, HD * k : HD * k + HD]
                for j in range(4):
                    qo_ref[2 * j + k, b, 8 * r : 8 * r + 8] = part


def pair_kernel(keep_ref, got_ref, hw_ref, ow_hbm, kv_ref, ow_ref, full_ref, sem):
    copy = pltpu.make_async_copy(ow_hbm.at[pl.ds(lax.axis_index("h") * HD, HD)], ow_ref, sem)
    copy.start()
    kv_ref[0, 0:528] = keep_ref[...]
    kv_ref[1, 0:528] = got_ref[...]
    full_ref[...] = jnp.zeros_like(full_ref)
    share = 160 * lax.rem(lax.axis_index("z"), 2)
    for m in range(16):
        full_ref[pl.ds(pl.multiple_of(320 * m + share, 16), 160)] = hw_ref[m]
    copy.wait()
    both = jnp.dot(ow_ref[...], full_ref[...], preferred_element_type=F32)
    both = both.T.astype(BF16)
    for k in range(2):
        for a in range(2):
            at = 32 * a + 16 * k
            kv_ref[k, 528 + 16 * a : 544 + 16 * a] = both[at : at + 16]


def split_kernel(far_ref, keep_ref, give_ref):
    first = lax.axis_index("h") == 0
    one, two = far_ref[:, 0:HD], far_ref[:, HD : 2 * HD]
    keep_ref[...] = jnp.where(first, one, two)
    give_ref[...] = jnp.where(first, two, one)


def attend(fm_ref, q_ref, planes, emit):
    lane = lax.broadcasted_iota(jnp.int32, (1, HD), 1)
    row_frame = lax.broadcasted_iota(jnp.int32, (256, 1), 0) % 128 // 32
    sources = []
    for kv_refs, plane in planes:
        frame = (plane % NZ) // 4
        block_bias = jnp.zeros((256, 1), F32)
        for f in range(FR):
            here = jnp.where(fm_ref[f, frame] == 1, 0.0, NEG)
            block_bias = jnp.where(row_frame == f, here, block_bias)
        block_bias = jnp.broadcast_to(block_bias, (256, 128))
        for kv_ref in kv_refs:
            filled = kv_ref[512:528, :].astype(F32)[0:1]
            cache_bias = jnp.where(lane.astype(F32) < filled, 0.0, NEG)
            sources.append((kv_ref, cache_bias, block_bias))

    def block(step, carry):
        q = jnp.concatenate([q_ref[:, 2 * step + i].reshape(128, HD) for i in range(2)], axis=0)
        scores = []
        for kv_ref, cache_bias, block_bias in sources:
            raw = dot_nt(q, kv_ref[0:256, :]) * C2
            bias = jnp.concatenate(
                [jnp.broadcast_to(cache_bias, (256, 128)), block_bias], axis=1
            )
            scores.append(raw + bias)
        top = functools.reduce(jnp.maximum, scores)
        top = jnp.max(top, axis=1, keepdims=True)
        total = jnp.zeros((256, 256), F32)
        acc = jnp.zeros((256, HD), F32)
        for score, (kv_ref, _, _) in zip(scores, sources):
            weights = jnp.exp2(score - top)
            total = total + weights
            acc = acc + jnp.dot(
                weights.astype(BF16), kv_ref[256:512, :], preferred_element_type=F32
            )
        total = jnp.sum(total, axis=1, keepdims=True)
        attended = (acc / total).astype(BF16)
        level = top + jnp.log2(total)
        for i in range(2):
            here = slice(128 * i, 128 * i + 128)
            turned = jnp.broadcast_to(level[here], (128, 128)).T[0:8]
            emit(2 * step + i, attended[here], turned)
        return carry

    lax.fori_loop(0, 4, block, 0, unroll=4)


def first_kernel(fm_ref, q_ref, kv_ref, keep_ref, got_ref, out_ref, level_ref):
    z, core = lax.axis_index("z"), lax.rem(lax.axis_index("mp"), 2)

    def emit(b, attended, level):
        out_ref[b] = attended
        level_ref[b] = level

    planes = (([kv_ref.at[0], kv_ref.at[1]], z), ([keep_ref, got_ref], z + NZ - 2 + 4 * core))
    attend(fm_ref, q_ref, planes, emit)


def second_kernel(
    fm_ref,
    q_ref,
    own_ref,
    kv1_ref,
    kv2_ref,
    first_ref,
    first_level_ref,
    prev_ref,
    out_ref,
    pt_ref,
    level_ref,
):
    z = lax.axis_index("z")
    shares = [jnp.concatenate([ref[0, 528:560], ref[1, 528:560]], 0) for ref in (own_ref, kv1_ref)]
    both = (shares[0].astype(F32) + shares[1].astype(F32)).astype(BF16)
    part = lax.broadcasted_iota(jnp.int32, (8, 128), 0)

    def emit(b, attended, level):
        other = first_level_ref[b]
        top = jnp.maximum(level, other)
        share, other = jnp.exp2(level - top), jnp.exp2(other - top)
        whole = share + other
        here, there = dot_nt(both, attended), dot_nt(both, first_ref[b])
        pt_ref[b] = (share / whole)[0:1] * here + (other / whole)[0:1] * there
        level = top + jnp.log2(whole)
        high = level.astype(BF16).astype(F32)
        mid = (level - high).astype(BF16).astype(F32)
        low = level - high - mid
        level_ref[b] = jnp.where(
            part == 0, high, jnp.where(part == 1, mid, jnp.where(part == 2, low, 0.0))
        )

    halves = [[ref.at[0], ref.at[1]] for ref in (kv1_ref, kv2_ref)]
    attend(fm_ref, q_ref, ((halves[0], z + NZ - 1), (halves[1], z + 1)), emit)
    ship(prev_ref, pt_ref, level_ref, out_ref)


def ship(prev_ref, pt_ref, level_ref, out_ref):
    edge = [prev_ref[f, a, 3 * e : 3 * e + 1, :] for e in range(2) for f in range(2) for a in range(2)]
    edge = jnp.concatenate([x.astype(F32) for x in edge], axis=1)
    column = lax.broadcasted_iota(jnp.int32, (32, 128), 1) % 8
    few = column[0:8]
    part = lax.broadcasted_iota(jnp.int32, (8, 128), 0)
    for z in range(NZ):
        b, odd = z // 2, z % 2
        beside = b - 1 + 2 * odd
        low, high = pt_ref[b, 0:32], pt_ref[b, 32:64]
        if odd:
            main = jnp.where(column >= 4, low, pltpu.roll(high, 124, 1))
        else:
            main = jnp.where(column < 4, low, pltpu.roll(high, 4, 1))
        halo = jnp.zeros((8, 128), F32)
        level = level_ref[b]
        for q in range(4):
            if not odd or beside < 8:
                right = pt_ref[beside if odd else b, 8 * q : 8 * q + 8]
                right = pltpu.roll(right, (q if odd else q - 4) % 128, 1)
                halo = jnp.where(few == q, right, halo)
            if odd or beside >= 0:
                left = pt_ref[b if odd else beside, 32 + 8 * q : 40 + 8 * q]
                left = pltpu.roll(left, (q + 1 if odd else q - 3) % 128, 1)
                halo = jnp.where(few == 4 + q, left, halo)
        if 0 <= beside < 8:
            level = jnp.where(few == 7 - 7 * odd, level_ref[beside], level)
        level = jnp.where(part == 3, edge, level)
        out_ref[z] = jnp.concatenate([main, halo, level], axis=0).astype(BF16)


def spread_kernel(y_ref, prev_ref, out_ref, rows_ref):
    z, h, m = (lax.axis_index(axis) for axis in ("z", "h", "mp"))
    odd = lax.rem(z, 2)
    level = []
    for n in range(NZ):
        tail = y_ref[n, 32:48].astype(F32)
        level.append(tail[8:9] + tail[9:10] + tail[10:11])
    level = jnp.concatenate(level, axis=0)
    top = jnp.maximum(
        jnp.maximum(level[0:4], level[4:8]), jnp.maximum(level[8:12], level[12:16])
    )
    share = jnp.exp2(level - jnp.concatenate([top] * 4, axis=0))
    whole = share[0:4] + share[4:8] + share[8:12] + share[12:16]
    share = share / jnp.concatenate([whole] * 4, axis=0)
    column = lax.broadcasted_iota(jnp.int32, (16, 128), 1) % 8
    main_share = jnp.where(odd == 1, pltpu.roll(share, 124, 1), share)
    main_share = jnp.where(column < 4, main_share, pltpu.roll(main_share, 4, 1))
    share = jnp.where(odd == 1, pltpu.roll(share, 4, 1), share)
    halo_share = jnp.zeros((16, 128), F32)
    for q in range(4):
        halo_share = jnp.where(column == q, pltpu.roll(share, (q - 4) % 128, 1), halo_share)
        halo_share = jnp.where(column == 4 + q, pltpu.roll(share, (q - 3) % 128, 1), halo_share)
    to = lax.broadcasted_iota(jnp.int32, (128, 128), 0)
    at = lax.broadcasted_iota(jnp.int32, (128, 128), 1)
    same = (at // 32 == to % 4) & ((at // 8) % 4 == to // 32)
    goal = 2 * ((to // 16) % 2) + (to // 4) % 4 - 1
    own = same & (goal >= 0) & (goal < 4)
    pick = [
        own & (at % 8 == goal + 4 * odd),
        own & (at % 8 == goal + 4 - 4 * odd),
        same & ((goal == 4) & (at % 8 < 4) | (goal == -1) & (at % 8 >= 4)),
    ]
    pick = jnp.concatenate([jnp.where(x, 1.0, 0.0).astype(BF16) for x in pick], axis=1)
    lane = lax.broadcasted_iota(jnp.int32, (1, 128), 1)
    earlier = []
    for c in range(2):
        for f in range(2):
            parts = [
                prev_ref[f, a, 2 * c + b : 2 * c + b + 1, :].astype(F32)
                for b in range(2)
                for a in range(2)
            ]
            earlier.append(jnp.concatenate([jnp.zeros((1, 64), F32)] + parts, axis=1))
    rim = y_ref[jnp.maximum(z - 1, 0), 32:48].astype(F32)[11:12]
    rim = jnp.where((z > 0) & (h == 1), rim, 0.0)
    for f in range(2):
        earlier.append(jnp.where(lane >= 96, pltpu.roll(rim, 32 - 32 * f, 1), 0.0))
    rim = y_ref[jnp.minimum(z + 1, NZ - 1), 32:48].astype(F32)[11:12]
    rim = jnp.where((z < NZ - 1) & (h == 0), rim, 0.0)
    for f in range(2):
        earlier.append(
            jnp.where((lane >= 64) & (lane < 96), pltpu.roll(rim, 64 - 32 * f, 1), 0.0)
        )
    to = lax.broadcasted_iota(jnp.int32, (32, 8), 0)
    item = lax.broadcasted_iota(jnp.int32, (32, 8), 1)
    cell = 2 * (to // 16) + (to // 4) % 4
    place = (item < 4) & (cell == 2 * h + item // 2 + 1)
    place = place | (item // 2 == 2) & (cell == 0) | (item // 2 == 3) & (cell == 5)
    place = jnp.where(place & (to % 4 == item % 2), 1.0, 0.0).astype(BF16)
    earlier = jnp.dot(
        place, jnp.concatenate(earlier, axis=0).astype(BF16), preferred_element_type=F32
    )
    few = column[0:8]
    blank = jnp.zeros((32, 128), F32)
    for r in range(4):
        main = jnp.zeros((32, 128), F32)
        halo = jnp.zeros((8, 128), F32)
        for g in range(4):
            n = 4 * g + r
            main = main + main_share[n : n + 1] * y_ref[n, 0:32].astype(F32)
            halo = halo + halo_share[n : n + 1] * y_ref[n, 32:48].astype(F32)[0:8]
        right = jnp.concatenate([jnp.where(few == q, halo, 0.0) for q in range(4)], axis=0)
        left = jnp.concatenate([jnp.where(few == 4 + q, halo, 0.0) for q in range(4)], axis=0)
        value = jnp.concatenate(
            [
                jnp.concatenate([main, blank, right], axis=1),
                jnp.concatenate([blank, main, left], axis=1),
                jnp.zeros((64, 384), F32),
            ],
            axis=0,
        )
        moved = dot_nt(pick, value.astype(BF16))
        for i in range(4):
            row = 4 * r + i
            rows_ref[row] = moved[32 * i : 32 * i + 32] + jnp.where(m == row, earlier, 0.0)
    below = lax.broadcasted_iota(jnp.int32, (32, 128), 1) % 32 < 16
    for row in range(16):
        under = rows_ref[row + 1] if row < 15 else jnp.zeros((32, 128), F32)
        over = rows_ref[row - 1] if row > 0 else jnp.zeros((32, 128), F32)
        beside = jnp.where(below, under, over).astype(BF16)
        own = rows_ref[row].astype(BF16)
        for k in range(2):
            out_ref[16 * k + row, 0:16] = own[16 * k : 16 * k + 16]
            out_ref[16 * k + row, 16:32] = beside[16 * k : 16 * k + 16]


def decode_kernel(r_ref, w_ref, bias_ref, gain_ref, out_ref, z_ref, taps_ref):
    nothing = jnp.zeros((16, CH), BF16)
    for a in range(2):
        for b in range(2):
            for dt in range(3):
                for k in range(16):
                    i, j, pb, pa = k // 8, k // 4 % 2, k // 2 % 2, k % 2
                    dy, dx = 2 * i + pa + a - 1, 2 * j + pb + b - 1
                    inside = 0 <= dy < 3 and 0 <= dx < 3
                    tap = w_ref[dt, dy, dx] if inside else nothing
                    taps_ref[a, b, dt, 16 * k : 16 * k + 16] = tap
    total = jnp.zeros((32, 128), F32)
    for s in range(32):
        total = total + r_ref[s].astype(F32)
    total = total.astype(BF16).astype(F32)
    z_ref[...] = jnp.zeros_like(z_ref)
    for dr in range(2):
        for cc in range(4):
            at = dr * 16 + cc * 4
            z_ref[dr, cc * 6 + 2 : cc * 6 + 6] = total[at : at + 4, 0:64]
            z_ref[dr, cc * 6 : cc * 6 + 2] = total[at : at + 2, 64:128]
    for a in range(2):
        for b in range(2):
            conv = jnp.zeros((16, CH), F32)
            for dt in range(3):
                pieces = []
                for i in range(2):
                    for j in range(2):
                        start = (b + j) * 6 + dt
                        pieces.append(z_ref[(a + i + 1) % 2, start : start + 16])
                lhs = jnp.concatenate(pieces, axis=1).astype(BF16)
                conv = conv + jnp.dot(lhs, taps_ref[a, b, dt], preferred_element_type=F32)
            conv = conv + bias_ref[...].reshape(1, CH)
            meansq = jnp.mean(conv * conv, axis=1, keepdims=True)
            normed = conv * lax.rsqrt(meansq + 1e-06) * gain_ref[...].reshape(1, CH)
            decoded = (normed / (1.0 + jnp.exp(-normed))).astype(BF16)
            for c in range(2):
                for f in range(FR):
                    out_ref[f, a, 2 * c + b] = decoded[c * 6 + f]


def body(
    queries,
    stretch_keys,
    stretch_values,
    cache_keys,
    cache_values,
    cache_lengths,
    frame_mask,
    out_weight,
    head_weight,
    previous_latent,
    conv_weight,
    conv_bias,
    norm_gain,
):
    z = lax.axis_index("z")
    vmem = pl.BlockSpec(memory_space=pltpu.VMEM)
    whole = pl.BlockSpec()
    hbm = pl.BlockSpec(memory_space=pltpu.HBM)
    smem = pl.BlockSpec(memory_space=pltpu.SMEM)

    def call(kernel, name, outs, specs, scratch=(), limit=16, **kw):
        shapes = [jax.ShapeDtypeStruct(shape, kind) for shape, kind in outs]
        return pl.pallas_call(
            kernel,
            out_shape=shapes if len(shapes) > 1 else shapes[0],
            in_specs=specs,
            out_specs=[vmem] * len(shapes) if len(shapes) > 1 else vmem,
            scratch_shapes=scratch,
            compiler_params=pltpu.CompilerParams(vmem_limit_bytes=limit * 1024 * 1024),
            name=name,
            **kw,
        )

    keep, give, raw, q = call(
        pack_kernel,
        "pack",
        (((528, HD), BF16), ((528, HD), BF16), ((528, 2 * HD), BF16), ((8, 8, 16, HD), BF16)),
        [hbm] * 6,
        [
            pltpu.VMEM((5, 128, 2 * HD), BF16),
            pltpu.SMEM((1,), jnp.int32),
            pltpu.SemaphoreType.DMA((6,)),
        ],
        limit=60,
    )(cache_lengths, queries, cache_keys, stretch_keys, cache_values, stretch_values)
    def swap(x):
        return lax.ppermute(x, "h", [(0, 1), (1, 0)])

    got = swap(give)
    far = lax.ppermute(
        raw,
        ("z", "mp"),
        [(16 * i + j, 16 * ((i + (2 if j % 2 == 0 else 14)) % NZ) + j) for i in range(NZ) for j in range(16)],
    )
    hw = lax.dynamic_slice_in_dim(head_weight, 160 * (z % 2), 160, 0)
    hw = lax.all_to_all(jnp.broadcast_to(hw[None], (16, 160, 64)), "mp", 0, 0, tiled=True)
    q, hw = lax.optimization_barrier((q, hw))
    q = lax.all_to_all(q, ("z", "h"), 0, 0, tiled=True, axis_index_groups=FAR)
    kv = call(
        pair_kernel,
        "pair",
        (((2, 560, HD), BF16),),
        [vmem] * 3 + [hbm],
        [pltpu.VMEM((HD, 5120), BF16), pltpu.VMEM((5120, 64), BF16), pltpu.SemaphoreType.DMA],
        limit=52,
        cost_estimate=pl.CostEstimate(flops=0, bytes_accessed=10**6, transcendentals=0),
    )(keep, got, hw, out_weight)
    up = lax.ppermute(kv, "z", [(i, (i + 1) % NZ) for i in range(NZ)])
    down = lax.ppermute(kv, "z", [((i + 1) % NZ, i) for i in range(NZ)])
    cost = pl.CostEstimate(flops=10**10, bytes_accessed=10**6, transcendentals=10**6)
    far_keep, far_give = call(
        split_kernel,
        "split",
        (((528, HD), BF16), ((528, HD), BF16)),
        [vmem],
        cost_estimate=pl.CostEstimate(flops=10**10, bytes_accessed=10**6, transcendentals=0),
    )(far)
    far_got = swap(far_give)
    first = call(
        first_kernel,
        "first",
        (((8, 128, HD), BF16), ((8, 8, 128), F32)),
        [smem] + [vmem] * 4,
        cost_estimate=cost,
    )(frame_mask, q, kv, far_keep, far_got)
    partial = call(
        second_kernel,
        "second",
        (((NZ, 48, 128), BF16),),
        [smem] + [vmem] * 7,
        [pltpu.VMEM((8, 64, 128), F32), pltpu.VMEM((8, 8, 128), F32)],
        cost_estimate=cost,
    )(frame_mask, q, kv, up, down, *first, previous_latent)
    partial = lax.all_to_all(partial, "z", 0, 0, tiled=True)
    spread = call(spread_kernel, "spread", (((32, 32, 128), BF16),), [vmem, whole], [pltpu.VMEM((16, 32, 128), F32)])(
        partial, previous_latent
    )
    spread = lax.all_to_all(spread, ("h", "mp"), 0, 0, tiled=True)
    return call(
        decode_kernel,
        "decode",
        (((FR, 2, 4, CH), BF16),),
        [vmem] + [whole] * 3,
        [pltpu.VMEM((2, 40, 64), F32), pltpu.VMEM((2, 2, 3, 256, CH), BF16)],
    )(spread, conv_weight, conv_bias, norm_gain)


def solution(mesh):
    fine = Mesh(mesh.devices.reshape(NZ, 2, 16), ("z", "h", "mp"))
    seq = ("z", "h")
    return jax.shard_map(
        body,
        mesh=fine,
        in_specs=(
            P(seq, "mp"),
            P(seq, "mp"),
            P(seq, "mp"),
            P(seq, "mp"),
            P(seq, "mp"),
            P(seq),
            P(),
            P("mp", None),
            P("mp", None),
            P(None, "mp", seq, None),
            P(),
            P(),
            P(),
        ),
        out_specs=P(None, "mp", seq, None),
        check_vma=False,
    )
```

```python
import functools
import math

import jax
import jax.numpy as jnp
from jax import lax
from jax.experimental import pallas as pl
from jax.experimental.pallas import tpu as pltpu
from jax.sharding import Mesh, PartitionSpec as P

HD = 128
LATC = 16
CH = 384
FR = 4
NZ = 16
NEG = -1e30
C2 = math.log2(math.e) / math.sqrt(HD)
F32 = jnp.float32
BF16 = jnp.bfloat16
FAR = [[(4 * j + i) * 2 + k for j in range(4) for k in range(2)] for i in range(4)]
NT = (((1,), (1,)), ((), ()))


def dot_nt(a, b):
    return lax.dot_general(a, b, NT, preferred_element_type=F32)


def pack_kernel(
    len_hbm, q_hbm, ck_hbm, sk_hbm, cv_hbm, sv_hbm, keep_ref, give_ref, raw_ref, qo_ref, buf, len_ref, sems
):
    copies = []
    for n, ref in enumerate((ck_hbm, sk_hbm, cv_hbm, sv_hbm, q_hbm)):
        copies.append(pltpu.make_async_copy(ref, buf.at[n], sems.at[n]))
        copies[n].start()
    length = pltpu.make_async_copy(len_hbm, len_ref, sems.at[5])
    length.start()
    first = lax.axis_index("h") == 0
    length.wait()
    filled = (jnp.zeros((16, HD), F32) + len_ref[0].astype(F32)).astype(BF16)
    keep_ref[512:528] = filled
    give_ref[512:528] = filled
    raw_ref[512:528] = jnp.concatenate([filled, filled], axis=1)
    for n in range(4):
        copies[n].wait()
        raw_ref[128 * n : 128 * n + 128] = buf[n]
        one, two = buf[n, :, 0:HD], buf[n, :, HD : 2 * HD]
        keep_ref[128 * n : 128 * n + 128] = jnp.where(first, one, two)
        give_ref[128 * n : 128 * n + 128] = jnp.where(first, two, one)
    copies[4].wait()
    for n in range(4):
        above = buf[4, 16 * n : 16 * n + 16, :].astype(F32)
        under = buf[4, 64 + 16 * n : 80 + 16 * n, :].astype(F32)
        for b in range(2):
            here = slice(8 * b, 8 * b + 8)
            rows = jnp.concatenate([above[here], under[here]], axis=0).astype(BF16)
            for k in range(2):
                for j in range(4):
                    qo_ref[2 * j + k, 2 * n + b] = rows[:, HD * k : HD * k + HD]


def pair_kernel(keep_ref, got_ref, hw_ref, ow_hbm, kv_ref, ow_ref, full_ref, sem):
    copy = pltpu.make_async_copy(ow_hbm.at[pl.ds(lax.axis_index("h") * HD, HD)], ow_ref, sem)
    copy.start()
    kv_ref[0, 0:528] = keep_ref[...]
    kv_ref[1, 0:528] = got_ref[...]
    full_ref[...] = jnp.zeros_like(full_ref)
    share = 160 * lax.rem(lax.axis_index("z"), 2)
    for m in range(16):
        full_ref[pl.ds(pl.multiple_of(320 * m + share, 16), 160)] = hw_ref[m]
    copy.wait()
    both = jnp.dot(ow_ref[...], full_ref[...], preferred_element_type=F32)
    both = both.T.astype(BF16)
    for k in range(2):
        for a in range(2):
            at = 32 * a + 16 * k
            kv_ref[k, 528 + 16 * a : 544 + 16 * a] = both[at : at + 16]


def split_kernel(far_ref, keep_ref, give_ref):
    first = lax.axis_index("h") == 0
    one, two = far_ref[:, 0:HD], far_ref[:, HD : 2 * HD]
    keep_ref[...] = jnp.where(first, one, two)
    give_ref[...] = jnp.where(first, two, one)


def attend(fm_ref, q_ref, planes, emit):
    lane = lax.broadcasted_iota(jnp.int32, (1, HD), 1)
    row_frame = lax.broadcasted_iota(jnp.int32, (256, 1), 0) % 128 // 32
    sources = []
    for kv_refs, plane in planes:
        frame = (plane % NZ) // 4
        block_bias = jnp.zeros((256, 1), F32)
        for f in range(FR):
            here = jnp.where(fm_ref[f, frame] == 1, 0.0, NEG)
            block_bias = jnp.where(row_frame == f, here, block_bias)
        block_bias = jnp.broadcast_to(block_bias, (256, 128))
        for kv_ref in kv_refs:
            filled = kv_ref[512:528, :].astype(F32)[0:1]
            cache_bias = jnp.where(lane.astype(F32) < filled, 0.0, NEG)
            sources.append((kv_ref, cache_bias, block_bias))

    def block(step, carry):
        q = jnp.concatenate([q_ref[:, 2 * step + i].reshape(128, HD) for i in range(2)], axis=0)
        scores = []
        for kv_ref, cache_bias, block_bias in sources:
            raw = dot_nt(q, kv_ref[0:256, :]) * C2
            bias = jnp.concatenate(
                [jnp.broadcast_to(cache_bias, (256, 128)), block_bias], axis=1
            )
            scores.append(raw + bias)
        top = functools.reduce(jnp.maximum, scores)
        top = jnp.max(top, axis=1, keepdims=True)
        total = jnp.zeros((256, 256), F32)
        acc = jnp.zeros((256, HD), F32)
        for score, (kv_ref, _, _) in zip(scores, sources):
            weights = jnp.exp2(score - top)
            total = total + weights
            acc = acc + jnp.dot(
                weights.astype(BF16), kv_ref[256:512, :], preferred_element_type=F32
            )
        total = jnp.sum(total, axis=1, keepdims=True)
        attended = (acc / total).astype(BF16)
        level = top + jnp.log2(total)
        for i in range(2):
            here = slice(128 * i, 128 * i + 128)
            turned = jnp.broadcast_to(level[here], (128, 128)).T[0:8]
            emit(2 * step + i, attended[here], turned)
        return carry

    lax.fori_loop(0, 4, block, 0, unroll=4)


def first_kernel(fm_ref, q_ref, kv_ref, keep_ref, got_ref, out_ref, level_ref):
    z, core = lax.axis_index("z"), lax.rem(lax.axis_index("mp"), 2)

    def emit(b, attended, level):
        out_ref[b] = attended
        level_ref[b] = level

    planes = (([kv_ref.at[0], kv_ref.at[1]], z), ([keep_ref, got_ref], z + NZ - 2 + 4 * core))
    attend(fm_ref, q_ref, planes, emit)


def second_kernel(
    fm_ref,
    q_ref,
    own_ref,
    kv1_ref,
    kv2_ref,
    first_ref,
    first_level_ref,
    prev_ref,
    out_ref,
    pt_ref,
    level_ref,
):
    z = lax.axis_index("z")
    shares = [jnp.concatenate([ref[0, 528:560], ref[1, 528:560]], 0) for ref in (own_ref, kv1_ref)]
    both = (shares[0].astype(F32) + shares[1].astype(F32)).astype(BF16)
    part = lax.broadcasted_iota(jnp.int32, (8, 128), 0)

    def emit(b, attended, level):
        other = first_level_ref[b]
        top = jnp.maximum(level, other)
        share, other = jnp.exp2(level - top), jnp.exp2(other - top)
        whole = share + other
        here, there = dot_nt(both, attended), dot_nt(both, first_ref[b])
        pt_ref[b] = (share / whole)[0:1] * here + (other / whole)[0:1] * there
        level = top + jnp.log2(whole)
        high = level.astype(BF16).astype(F32)
        mid = (level - high).astype(BF16).astype(F32)
        low = level - high - mid
        level_ref[b] = jnp.where(
            part == 0, high, jnp.where(part == 1, mid, jnp.where(part == 2, low, 0.0))
        )

    halves = [[ref.at[0], ref.at[1]] for ref in (kv1_ref, kv2_ref)]
    attend(fm_ref, q_ref, ((halves[0], z + NZ - 1), (halves[1], z + 1)), emit)
    ship(prev_ref, pt_ref, level_ref, out_ref)


def ship(prev_ref, pt_ref, level_ref, out_ref):
    cells = [[prev_ref[f, a].astype(F32) for a in range(2)] for f in range(2)]
    edge = [cells[f][a][3 * e : 3 * e + 1] for e in range(2) for f in range(2) for a in range(2)]
    edge = jnp.concatenate(edge, axis=1)
    column = lax.broadcasted_iota(jnp.int32, (32, 128), 1) % 8
    few = column[0:8]
    part = lax.broadcasted_iota(jnp.int32, (8, 128), 0)
    for z in range(NZ):
        b, odd = z // 2, z % 2
        beside = b - 1 + 2 * odd
        low, high = pt_ref[b, 0:32], pt_ref[b, 32:64]
        if odd:
            main = jnp.where(column >= 4, low, pltpu.roll(high, 124, 1))
        else:
            main = jnp.where(column < 4, low, pltpu.roll(high, 4, 1))
        halo = jnp.zeros((8, 128), F32)
        level = level_ref[b]
        for q in range(4):
            if not odd or beside < 8:
                right = pt_ref[beside if odd else b, 8 * q : 8 * q + 8]
                right = pltpu.roll(right, (q if odd else q - 4) % 128, 1)
                halo = jnp.where(few == q, right, halo)
            if odd or beside >= 0:
                left = pt_ref[b if odd else beside, 32 + 8 * q : 40 + 8 * q]
                left = pltpu.roll(left, (q + 1 if odd else q - 3) % 128, 1)
                halo = jnp.where(few == 4 + q, left, halo)
        if 0 <= beside < 8:
            level = jnp.where(few == 7 - 7 * odd, level_ref[beside], level)
        level = jnp.where(part == 3, edge, level)
        out_ref[z] = jnp.concatenate([main, halo, level], axis=0).astype(BF16)


def spread_kernel(y_ref, prev_ref, out_ref, rows_ref):
    z, h, m = (lax.axis_index(axis) for axis in ("z", "h", "mp"))
    odd = lax.rem(z, 2)
    level = []
    for n in range(NZ):
        tail = y_ref[n, 32:48].astype(F32)
        level.append(tail[8:9] + tail[9:10] + tail[10:11])
    level = jnp.concatenate(level, axis=0)
    top = jnp.maximum(
        jnp.maximum(level[0:4], level[4:8]), jnp.maximum(level[8:12], level[12:16])
    )
    share = jnp.exp2(level - jnp.concatenate([top] * 4, axis=0))
    whole = share[0:4] + share[4:8] + share[8:12] + share[12:16]
    share = share / jnp.concatenate([whole] * 4, axis=0)
    column = lax.broadcasted_iota(jnp.int32, (16, 128), 1) % 8
    main_share = jnp.where(odd == 1, pltpu.roll(share, 124, 1), share)
    main_share = jnp.where(column < 4, main_share, pltpu.roll(main_share, 4, 1))
    share = jnp.where(odd == 1, pltpu.roll(share, 4, 1), share)
    halo_share = jnp.zeros((16, 128), F32)
    for q in range(4):
        halo_share = jnp.where(column == q, pltpu.roll(share, (q - 4) % 128, 1), halo_share)
        halo_share = jnp.where(column == 4 + q, pltpu.roll(share, (q - 3) % 128, 1), halo_share)
    to = lax.broadcasted_iota(jnp.int32, (128, 128), 0)
    at = lax.broadcasted_iota(jnp.int32, (128, 128), 1)
    same = (at // 32 == to % 4) & ((at // 8) % 4 == to // 32)
    goal = 2 * ((to // 16) % 2) + (to // 4) % 4 - 1
    own = same & (goal >= 0) & (goal < 4)
    pick = [
        own & (at % 8 == goal + 4 * odd),
        own & (at % 8 == goal + 4 - 4 * odd),
        same & ((goal == 4) & (at % 8 < 4) | (goal == -1) & (at % 8 >= 4)),
    ]
    pick = jnp.concatenate([jnp.where(x, 1.0, 0.0).astype(BF16) for x in pick], axis=1)
    lane = lax.broadcasted_iota(jnp.int32, (1, 128), 1)
    cells = [[prev_ref[f, a].astype(F32) for a in range(2)] for f in range(2)]
    earlier = []
    for c in range(2):
        for f in range(2):
            parts = [
                cells[f][a][2 * c + b : 2 * c + b + 1] for b in range(2) for a in range(2)
            ]
            earlier.append(jnp.concatenate([jnp.zeros((1, 64), F32)] + parts, axis=1))
    rim = y_ref[jnp.maximum(z - 1, 0), 32:48].astype(F32)[11:12]
    rim = jnp.where((z > 0) & (h == 1), rim, 0.0)
    for f in range(2):
        earlier.append(jnp.where(lane >= 96, pltpu.roll(rim, 32 - 32 * f, 1), 0.0))
    rim = y_ref[jnp.minimum(z + 1, NZ - 1), 32:48].astype(F32)[11:12]
    rim = jnp.where((z < NZ - 1) & (h == 0), rim, 0.0)
    for f in range(2):
        earlier.append(
            jnp.where((lane >= 64) & (lane < 96), pltpu.roll(rim, 64 - 32 * f, 1), 0.0)
        )
    to = lax.broadcasted_iota(jnp.int32, (32, 8), 0)
    item = lax.broadcasted_iota(jnp.int32, (32, 8), 1)
    cell = 2 * (to // 16) + (to // 4) % 4
    place = (item < 4) & (cell == 2 * h + item // 2 + 1)
    place = place | (item // 2 == 2) & (cell == 0) | (item // 2 == 3) & (cell == 5)
    place = jnp.where(place & (to % 4 == item % 2), 1.0, 0.0).astype(BF16)
    earlier = jnp.dot(
        place, jnp.concatenate(earlier, axis=0).astype(BF16), preferred_element_type=F32
    )
    few = column[0:8]
    blank = jnp.zeros((32, 128), F32)
    for r in range(4):
        main = jnp.zeros((32, 128), F32)
        halo = jnp.zeros((8, 128), F32)
        for g in range(4):
            n = 4 * g + r
            main = main + main_share[n : n + 1] * y_ref[n, 0:32].astype(F32)
            halo = halo + halo_share[n : n + 1] * y_ref[n, 32:48].astype(F32)[0:8]
        right = jnp.concatenate([jnp.where(few == q, halo, 0.0) for q in range(4)], axis=0)
        left = jnp.concatenate([jnp.where(few == 4 + q, halo, 0.0) for q in range(4)], axis=0)
        value = jnp.concatenate(
            [
                jnp.concatenate([main, blank, right], axis=1),
                jnp.concatenate([blank, main, left], axis=1),
                jnp.zeros((64, 384), F32),
            ],
            axis=0,
        )
        moved = dot_nt(pick, value.astype(BF16))
        for i in range(4):
            row = 4 * r + i
            rows_ref[row] = moved[32 * i : 32 * i + 32] + jnp.where(m == row, earlier, 0.0)
    below = lax.broadcasted_iota(jnp.int32, (32, 128), 1) % 32 < 16
    for row in range(16):
        under = rows_ref[row + 1] if row < 15 else jnp.zeros((32, 128), F32)
        over = rows_ref[row - 1] if row > 0 else jnp.zeros((32, 128), F32)
        beside = jnp.where(below, under, over).astype(BF16)
        own = rows_ref[row].astype(BF16)
        for k in range(2):
            out_ref[16 * k + row, 0:16] = own[16 * k : 16 * k + 16]
            out_ref[16 * k + row, 16:32] = beside[16 * k : 16 * k + 16]


def decode_kernel(r_ref, w_ref, bias_ref, gain_ref, out_ref, z_ref, taps_ref):
    nothing = jnp.zeros((16, CH), BF16)
    for a in range(2):
        for b in range(2):
            for dt in range(3):
                for k in range(16):
                    i, j, pb, pa = k // 8, k // 4 % 2, k // 2 % 2, k % 2
                    dy, dx = 2 * i + pa + a - 1, 2 * j + pb + b - 1
                    inside = 0 <= dy < 3 and 0 <= dx < 3
                    tap = w_ref[dt, dy, dx] if inside else nothing
                    taps_ref[a, b, dt, 16 * k : 16 * k + 16] = tap
    total = jnp.zeros((32, 128), F32)
    for s in range(32):
        total = total + r_ref[s].astype(F32)
    total = total.astype(BF16).astype(F32)
    z_ref[...] = jnp.zeros_like(z_ref)
    for dr in range(2):
        for cc in range(4):
            at = dr * 16 + cc * 4
            z_ref[dr, cc * 6 + 2 : cc * 6 + 6] = total[at : at + 4, 0:64]
            z_ref[dr, cc * 6 : cc * 6 + 2] = total[at : at + 2, 64:128]
    for a in range(2):
        for b in range(2):
            conv = jnp.zeros((16, CH), F32)
            for dt in range(3):
                pieces = []
                for i in range(2):
                    for j in range(2):
                        start = (b + j) * 6 + dt
                        pieces.append(z_ref[(a + i + 1) % 2, start : start + 16])
                lhs = jnp.concatenate(pieces, axis=1).astype(BF16)
                conv = conv + jnp.dot(lhs, taps_ref[a, b, dt], preferred_element_type=F32)
            conv = conv + bias_ref[...].reshape(1, CH)
            meansq = jnp.mean(conv * conv, axis=1, keepdims=True)
            normed = conv * lax.rsqrt(meansq + 1e-06) * gain_ref[...].reshape(1, CH)
            decoded = (normed / (1.0 + jnp.exp(-normed))).astype(BF16)
            for c in range(2):
                for f in range(FR):
                    out_ref[f, a, 2 * c + b] = decoded[c * 6 + f]


def body(
    queries,
    stretch_keys,
    stretch_values,
    cache_keys,
    cache_values,
    cache_lengths,
    frame_mask,
    out_weight,
    head_weight,
    previous_latent,
    conv_weight,
    conv_bias,
    norm_gain,
):
    z = lax.axis_index("z")
    vmem = pl.BlockSpec(memory_space=pltpu.VMEM)
    whole = pl.BlockSpec()
    hbm = pl.BlockSpec(memory_space=pltpu.HBM)
    smem = pl.BlockSpec(memory_space=pltpu.SMEM)

    def call(kernel, name, outs, specs, scratch=(), limit=16, **kw):
        shapes = [jax.ShapeDtypeStruct(shape, kind) for shape, kind in outs]
        return pl.pallas_call(
            kernel,
            out_shape=shapes if len(shapes) > 1 else shapes[0],
            in_specs=specs,
            out_specs=[vmem] * len(shapes) if len(shapes) > 1 else vmem,
            scratch_shapes=scratch,
            compiler_params=pltpu.CompilerParams(vmem_limit_bytes=limit * 1024 * 1024),
            name=name,
            **kw,
        )

    keep, give, raw, q = call(
        pack_kernel,
        "pack",
        (((528, HD), BF16), ((528, HD), BF16), ((528, 2 * HD), BF16), ((8, 8, 16, HD), BF16)),
        [hbm] * 6,
        [
            pltpu.VMEM((5, 128, 2 * HD), BF16),
            pltpu.SMEM((1,), jnp.int32),
            pltpu.SemaphoreType.DMA((6,)),
        ],
        limit=60,
    )(cache_lengths, queries, cache_keys, stretch_keys, cache_values, stretch_values)
    def swap(x):
        return lax.ppermute(x, "h", [(0, 1), (1, 0)])

    got = swap(give)
    far = lax.ppermute(
        raw,
        ("z", "mp"),
        [(16 * i + j, 16 * ((i + (2 if j % 2 == 0 else 14)) % NZ) + j) for i in range(NZ) for j in range(16)],
    )
    hw = lax.dynamic_slice_in_dim(head_weight, 160 * (z % 2), 160, 0)
    hw = lax.all_to_all(jnp.broadcast_to(hw[None], (16, 160, 64)), "mp", 0, 0, tiled=True)
    q, hw = lax.optimization_barrier((q, hw))
    q = lax.all_to_all(q, ("z", "h"), 0, 0, tiled=True, axis_index_groups=FAR)
    kv = call(
        pair_kernel,
        "pair",
        (((2, 560, HD), BF16),),
        [vmem] * 3 + [hbm],
        [pltpu.VMEM((HD, 5120), BF16), pltpu.VMEM((5120, 64), BF16), pltpu.SemaphoreType.DMA],
        limit=52,
        cost_estimate=pl.CostEstimate(flops=0, bytes_accessed=10**6, transcendentals=0),
    )(keep, got, hw, out_weight)
    up = lax.ppermute(kv, "z", [(i, (i + 1) % NZ) for i in range(NZ)])
    down = lax.ppermute(kv, "z", [((i + 1) % NZ, i) for i in range(NZ)])
    cost = pl.CostEstimate(flops=10**10, bytes_accessed=10**6, transcendentals=10**6)
    far_keep, far_give = call(
        split_kernel,
        "split",
        (((528, HD), BF16), ((528, HD), BF16)),
        [vmem],
        cost_estimate=pl.CostEstimate(flops=10**10, bytes_accessed=10**6, transcendentals=0),
    )(far)
    far_got = swap(far_give)
    first = call(
        first_kernel,
        "first",
        (((8, 128, HD), BF16), ((8, 8, 128), F32)),
        [smem] + [vmem] * 4,
        cost_estimate=cost,
    )(frame_mask, q, kv, far_keep, far_got)
    partial = call(
        second_kernel,
        "second",
        (((NZ, 48, 128), BF16),),
        [smem] + [vmem] * 7,
        [pltpu.VMEM((8, 64, 128), F32), pltpu.VMEM((8, 8, 128), F32)],
        cost_estimate=cost,
    )(frame_mask, q, kv, up, down, *first, previous_latent)
    partial = lax.all_to_all(partial, "z", 0, 0, tiled=True)
    spread = call(spread_kernel, "spread", (((32, 32, 128), BF16),), [vmem, whole], [pltpu.VMEM((16, 32, 128), F32)])(
        partial, previous_latent
    )
    spread = lax.all_to_all(spread, ("h", "mp"), 0, 0, tiled=True)
    return call(
        decode_kernel,
        "decode",
        (((FR, 2, 4, CH), BF16),),
        [vmem] + [whole] * 3,
        [pltpu.VMEM((2, 40, 64), F32), pltpu.VMEM((2, 2, 3, 256, CH), BF16)],
    )(spread, conv_weight, conv_bias, norm_gain)


def solution(mesh):
    fine = Mesh(mesh.devices.reshape(NZ, 2, 16), ("z", "h", "mp"))
    seq = ("z", "h")
    return jax.shard_map(
        body,
        mesh=fine,
        in_specs=(
            P(seq, "mp"),
            P(seq, "mp"),
            P(seq, "mp"),
            P(seq, "mp"),
            P(seq, "mp"),
            P(seq),
            P(),
            P("mp", None),
            P("mp", None),
            P(None, "mp", seq, None),
            P(),
            P(),
            P(),
        ),
        out_specs=P(None, "mp", seq, None),
        check_vma=False,
    )
```

```python
import functools
import math

import jax
import jax.numpy as jnp
from jax import lax
from jax.experimental import pallas as pl
from jax.experimental.pallas import tpu as pltpu
from jax.sharding import Mesh, PartitionSpec as P

HD = 128
LATC = 16
CH = 384
FR = 4
NZ = 16
NEG = -1e30
C2 = math.log2(math.e) / math.sqrt(HD)
F32 = jnp.float32
BF16 = jnp.bfloat16
FAR = [[(4 * j + i) * 2 + k for j in range(4) for k in range(2)] for i in range(4)]
NT = (((1,), (1,)), ((), ()))


def dot_nt(a, b):
    return lax.dot_general(a, b, NT, preferred_element_type=F32)


def pack_kernel(
    len_hbm, q_hbm, ck_hbm, sk_hbm, cv_hbm, sv_hbm, keep_ref, give_ref, raw_ref, qo_ref, buf, len_ref, sems
):
    copies = []
    for n, ref in enumerate((ck_hbm, sk_hbm, cv_hbm, sv_hbm, q_hbm)):
        copies.append(pltpu.make_async_copy(ref, buf.at[n], sems.at[n]))
        copies[n].start()
    length = pltpu.make_async_copy(len_hbm, len_ref, sems.at[5])
    length.start()
    first = lax.axis_index("h") == 0
    length.wait()
    filled = (jnp.zeros((16, HD), F32) + len_ref[0].astype(F32)).astype(BF16)
    keep_ref[512:528] = filled
    give_ref[512:528] = filled
    raw_ref[512:528] = jnp.concatenate([filled, filled], axis=1)
    for n in range(4):
        copies[n].wait()
        raw_ref[128 * n : 128 * n + 128] = buf[n]
        one, two = buf[n, :, 0:HD], buf[n, :, HD : 2 * HD]
        keep_ref[128 * n : 128 * n + 128] = jnp.where(first, one, two)
        give_ref[128 * n : 128 * n + 128] = jnp.where(first, two, one)
    copies[4].wait()
    for n in range(4):
        above = buf[4, 16 * n : 16 * n + 16, :].astype(F32)
        under = buf[4, 64 + 16 * n : 80 + 16 * n, :].astype(F32)
        for b in range(2):
            here = slice(8 * b, 8 * b + 8)
            rows = jnp.concatenate([above[here], under[here]], axis=0).astype(BF16)
            for k in range(2):
                for j in range(4):
                    qo_ref[2 * j + k, 2 * n + b] = rows[:, HD * k : HD * k + HD]


def pair_kernel(keep_ref, got_ref, hw_ref, ow_hbm, kv_ref, ow_ref, full_ref, sems):
    rows = pl.ds(lax.axis_index("h") * HD, HD)
    copies = []
    for n in range(4):
        part = slice(1280 * n, 1280 * n + 1280)
        copies.append(pltpu.make_async_copy(ow_hbm.at[rows, part], ow_ref.at[:, part], sems.at[n]))
        copies[n].start()
    kv_ref[0, 0:528] = keep_ref[...]
    kv_ref[1, 0:528] = got_ref[...]
    full_ref[...] = jnp.zeros_like(full_ref)
    share = 160 * lax.rem(lax.axis_index("z"), 2)
    for m in range(16):
        full_ref[pl.ds(pl.multiple_of(320 * m + share, 16), 160)] = hw_ref[m]
    both = jnp.zeros((HD, 64), F32)
    for n in range(4):
        copies[n].wait()
        part = slice(1280 * n, 1280 * n + 1280)
        both = both + jnp.dot(ow_ref[:, part], full_ref[part], preferred_element_type=F32)
    both = both.T.astype(BF16)
    for k in range(2):
        for a in range(2):
            at = 32 * a + 16 * k
            kv_ref[k, 528 + 16 * a : 544 + 16 * a] = both[at : at + 16]


def split_kernel(far_ref, keep_ref, give_ref):
    first = lax.axis_index("h") == 0
    one, two = far_ref[:, 0:HD], far_ref[:, HD : 2 * HD]
    keep_ref[...] = jnp.where(first, one, two)
    give_ref[...] = jnp.where(first, two, one)


def attend(fm_ref, q_ref, planes, emit):
    lane = lax.broadcasted_iota(jnp.int32, (1, HD), 1)
    row_frame = lax.broadcasted_iota(jnp.int32, (256, 1), 0) % 128 // 32
    sources = []
    for kv_refs, plane in planes:
        frame = (plane % NZ) // 4
        block_bias = jnp.zeros((256, 1), F32)
        for f in range(FR):
            here = jnp.where(fm_ref[f, frame] == 1, 0.0, NEG)
            block_bias = jnp.where(row_frame == f, here, block_bias)
        block_bias = jnp.broadcast_to(block_bias, (256, 128))
        for kv_ref in kv_refs:
            filled = kv_ref[512:528, :].astype(F32)[0:1]
            cache_bias = jnp.where(lane.astype(F32) < filled, 0.0, NEG)
            sources.append((kv_ref, cache_bias, block_bias))

    def block(step, carry):
        q = jnp.concatenate([q_ref[:, 2 * step + i].reshape(128, HD) for i in range(2)], axis=0)
        scores = []
        for kv_ref, cache_bias, block_bias in sources:
            raw = dot_nt(q, kv_ref[0:256, :]) * C2
            bias = jnp.concatenate(
                [jnp.broadcast_to(cache_bias, (256, 128)), block_bias], axis=1
            )
            scores.append(raw + bias)
        top = functools.reduce(jnp.maximum, scores)
        top = jnp.max(top, axis=1, keepdims=True)
        total = jnp.zeros((256, 256), F32)
        acc = jnp.zeros((256, HD), F32)
        for score, (kv_ref, _, _) in zip(scores, sources):
            weights = jnp.exp2(score - top)
            total = total + weights
            acc = acc + jnp.dot(
                weights.astype(BF16), kv_ref[256:512, :], preferred_element_type=F32
            )
        total = jnp.sum(total, axis=1, keepdims=True)
        attended = (acc / total).astype(BF16)
        level = top + jnp.log2(total)
        for i in range(2):
            here = slice(128 * i, 128 * i + 128)
            turned = jnp.broadcast_to(level[here], (128, 128)).T[0:8]
            emit(2 * step + i, attended[here], turned)
        return carry

    lax.fori_loop(0, 4, block, 0, unroll=4)


def first_kernel(fm_ref, q_ref, kv_ref, keep_ref, got_ref, out_ref, level_ref):
    z, core = lax.axis_index("z"), lax.rem(lax.axis_index("mp"), 2)

    def emit(b, attended, level):
        out_ref[b] = attended
        level_ref[b] = level

    planes = (([kv_ref.at[0], kv_ref.at[1]], z), ([keep_ref, got_ref], z + NZ - 2 + 4 * core))
    attend(fm_ref, q_ref, planes, emit)


def second_kernel(
    fm_ref,
    q_ref,
    own_ref,
    kv1_ref,
    kv2_ref,
    first_ref,
    first_level_ref,
    prev_ref,
    out_ref,
    pt_ref,
    level_ref,
):
    z = lax.axis_index("z")
    shares = [jnp.concatenate([ref[0, 528:560], ref[1, 528:560]], 0) for ref in (own_ref, kv1_ref)]
    both = (shares[0].astype(F32) + shares[1].astype(F32)).astype(BF16)
    part = lax.broadcasted_iota(jnp.int32, (8, 128), 0)

    def emit(b, attended, level):
        other = first_level_ref[b]
        top = jnp.maximum(level, other)
        share, other = jnp.exp2(level - top), jnp.exp2(other - top)
        whole = share + other
        here, there = dot_nt(both, attended), dot_nt(both, first_ref[b])
        pt_ref[b] = (share / whole)[0:1] * here + (other / whole)[0:1] * there
        level = top + jnp.log2(whole)
        high = level.astype(BF16).astype(F32)
        mid = (level - high).astype(BF16).astype(F32)
        low = level - high - mid
        level_ref[b] = jnp.where(
            part == 0, high, jnp.where(part == 1, mid, jnp.where(part == 2, low, 0.0))
        )

    halves = [[ref.at[0], ref.at[1]] for ref in (kv1_ref, kv2_ref)]
    attend(fm_ref, q_ref, ((halves[0], z + NZ - 1), (halves[1], z + 1)), emit)
    ship(prev_ref, pt_ref, level_ref, out_ref)


def ship(prev_ref, pt_ref, level_ref, out_ref):
    cells = [[prev_ref[f, a].astype(F32) for a in range(2)] for f in range(2)]
    edge = [cells[f][a][3 * e : 3 * e + 1] for e in range(2) for f in range(2) for a in range(2)]
    edge = jnp.concatenate(edge, axis=1)
    column = lax.broadcasted_iota(jnp.int32, (32, 128), 1) % 8
    few = column[0:8]
    part = lax.broadcasted_iota(jnp.int32, (8, 128), 0)
    for z in range(NZ):
        b, odd = z // 2, z % 2
        beside = b - 1 + 2 * odd
        low, high = pt_ref[b, 0:32], pt_ref[b, 32:64]
        if odd:
            main = jnp.where(column >= 4, low, pltpu.roll(high, 124, 1))
        else:
            main = jnp.where(column < 4, low, pltpu.roll(high, 4, 1))
        halo = jnp.zeros((8, 128), F32)
        level = level_ref[b]
        for q in range(4):
            if not odd or beside < 8:
                right = pt_ref[beside if odd else b, 8 * q : 8 * q + 8]
                right = pltpu.roll(right, (q if odd else q - 4) % 128, 1)
                halo = jnp.where(few == q, right, halo)
            if odd or beside >= 0:
                left = pt_ref[b if odd else beside, 32 + 8 * q : 40 + 8 * q]
                left = pltpu.roll(left, (q + 1 if odd else q - 3) % 128, 1)
                halo = jnp.where(few == 4 + q, left, halo)
        if 0 <= beside < 8:
            level = jnp.where(few == 7 - 7 * odd, level_ref[beside], level)
        level = jnp.where(part == 3, edge, level)
        out_ref[z] = jnp.concatenate([main, halo, level], axis=0).astype(BF16)


def spread_kernel(y_ref, prev_ref, out_ref, rows_ref):
    z, h, m = (lax.axis_index(axis) for axis in ("z", "h", "mp"))
    odd = lax.rem(z, 2)
    level = []
    for n in range(NZ):
        tail = y_ref[n, 32:48].astype(F32)
        level.append(tail[8:9] + tail[9:10] + tail[10:11])
    level = jnp.concatenate(level, axis=0)
    top = jnp.maximum(
        jnp.maximum(level[0:4], level[4:8]), jnp.maximum(level[8:12], level[12:16])
    )
    share = jnp.exp2(level - jnp.concatenate([top] * 4, axis=0))
    whole = share[0:4] + share[4:8] + share[8:12] + share[12:16]
    share = share / jnp.concatenate([whole] * 4, axis=0)
    column = lax.broadcasted_iota(jnp.int32, (16, 128), 1) % 8
    main_share = jnp.where(odd == 1, pltpu.roll(share, 124, 1), share)
    main_share = jnp.where(column < 4, main_share, pltpu.roll(main_share, 4, 1))
    share = jnp.where(odd == 1, pltpu.roll(share, 4, 1), share)
    halo_share = jnp.zeros((16, 128), F32)
    for q in range(4):
        halo_share = jnp.where(column == q, pltpu.roll(share, (q - 4) % 128, 1), halo_share)
        halo_share = jnp.where(column == 4 + q, pltpu.roll(share, (q - 3) % 128, 1), halo_share)
    to = lax.broadcasted_iota(jnp.int32, (128, 128), 0)
    at = lax.broadcasted_iota(jnp.int32, (128, 128), 1)
    same = (at // 32 == to % 4) & ((at // 8) % 4 == to // 32)
    goal = 2 * ((to // 16) % 2) + (to // 4) % 4 - 1
    own = same & (goal >= 0) & (goal < 4)
    pick = [
        own & (at % 8 == goal + 4 * odd),
        own & (at % 8 == goal + 4 - 4 * odd),
        same & ((goal == 4) & (at % 8 < 4) | (goal == -1) & (at % 8 >= 4)),
    ]
    pick = jnp.concatenate([jnp.where(x, 1.0, 0.0).astype(BF16) for x in pick], axis=1)
    lane = lax.broadcasted_iota(jnp.int32, (1, 128), 1)
    cells = [[prev_ref[f, a].astype(F32) for a in range(2)] for f in range(2)]
    earlier = []
    for c in range(2):
        for f in range(2):
            parts = [
                cells[f][a][2 * c + b : 2 * c + b + 1] for b in range(2) for a in range(2)
            ]
            earlier.append(jnp.concatenate([jnp.zeros((1, 64), F32)] + parts, axis=1))
    rim = y_ref[jnp.maximum(z - 1, 0), 32:48].astype(F32)[11:12]
    rim = jnp.where((z > 0) & (h == 1), rim, 0.0)
    for f in range(2):
        earlier.append(jnp.where(lane >= 96, pltpu.roll(rim, 32 - 32 * f, 1), 0.0))
    rim = y_ref[jnp.minimum(z + 1, NZ - 1), 32:48].astype(F32)[11:12]
    rim = jnp.where((z < NZ - 1) & (h == 0), rim, 0.0)
    for f in range(2):
        earlier.append(
            jnp.where((lane >= 64) & (lane < 96), pltpu.roll(rim, 64 - 32 * f, 1), 0.0)
        )
    to = lax.broadcasted_iota(jnp.int32, (32, 8), 0)
    item = lax.broadcasted_iota(jnp.int32, (32, 8), 1)
    cell = 2 * (to // 16) + (to // 4) % 4
    place = (item < 4) & (cell == 2 * h + item // 2 + 1)
    place = place | (item // 2 == 2) & (cell == 0) | (item // 2 == 3) & (cell == 5)
    place = jnp.where(place & (to % 4 == item % 2), 1.0, 0.0).astype(BF16)
    earlier = jnp.dot(
        place, jnp.concatenate(earlier, axis=0).astype(BF16), preferred_element_type=F32
    )
    few = column[0:8]
    blank = jnp.zeros((32, 128), F32)
    for r in range(4):
        main = jnp.zeros((32, 128), F32)
        halo = jnp.zeros((8, 128), F32)
        for g in range(4):
            n = 4 * g + r
            main = main + main_share[n : n + 1] * y_ref[n, 0:32].astype(F32)
            halo = halo + halo_share[n : n + 1] * y_ref[n, 32:48].astype(F32)[0:8]
        right = jnp.concatenate([jnp.where(few == q, halo, 0.0) for q in range(4)], axis=0)
        left = jnp.concatenate([jnp.where(few == 4 + q, halo, 0.0) for q in range(4)], axis=0)
        value = jnp.concatenate(
            [
                jnp.concatenate([main, blank, right], axis=1),
                jnp.concatenate([blank, main, left], axis=1),
                jnp.zeros((64, 384), F32),
            ],
            axis=0,
        )
        moved = dot_nt(pick, value.astype(BF16))
        for i in range(4):
            row = 4 * r + i
            rows_ref[row] = moved[32 * i : 32 * i + 32] + jnp.where(m == row, earlier, 0.0)
    below = lax.broadcasted_iota(jnp.int32, (32, 128), 1) % 32 < 16
    for row in range(16):
        under = rows_ref[row + 1] if row < 15 else jnp.zeros((32, 128), F32)
        over = rows_ref[row - 1] if row > 0 else jnp.zeros((32, 128), F32)
        beside = jnp.where(below, under, over).astype(BF16)
        own = rows_ref[row].astype(BF16)
        for k in range(2):
            out_ref[16 * k + row, 0:16] = own[16 * k : 16 * k + 16]
            out_ref[16 * k + row, 16:32] = beside[16 * k : 16 * k + 16]


def decode_kernel(r_ref, w_ref, bias_ref, gain_ref, out_ref, z_ref, taps_ref):
    nothing = jnp.zeros((16, CH), BF16)
    for a in range(2):
        for b in range(2):
            for dt in range(3):
                for k in range(16):
                    i, j, pb, pa = k // 8, k // 4 % 2, k // 2 % 2, k % 2
                    dy, dx = 2 * i + pa + a - 1, 2 * j + pb + b - 1
                    inside = 0 <= dy < 3 and 0 <= dx < 3
                    tap = w_ref[dt, dy, dx] if inside else nothing
                    taps_ref[a, b, dt, 16 * k : 16 * k + 16] = tap
    total = jnp.zeros((32, 128), F32)
    for s in range(32):
        total = total + r_ref[s].astype(F32)
    total = total.astype(BF16).astype(F32)
    z_ref[...] = jnp.zeros_like(z_ref)
    for dr in range(2):
        for cc in range(4):
            at = dr * 16 + cc * 4
            z_ref[dr, cc * 6 + 2 : cc * 6 + 6] = total[at : at + 4, 0:64]
            z_ref[dr, cc * 6 : cc * 6 + 2] = total[at : at + 2, 64:128]
    for a in range(2):
        for b in range(2):
            conv = jnp.zeros((16, CH), F32)
            for dt in range(3):
                pieces = []
                for i in range(2):
                    for j in range(2):
                        start = (b + j) * 6 + dt
                        pieces.append(z_ref[(a + i + 1) % 2, start : start + 16])
                lhs = jnp.concatenate(pieces, axis=1).astype(BF16)
                conv = conv + jnp.dot(lhs, taps_ref[a, b, dt], preferred_element_type=F32)
            conv = conv + bias_ref[...].reshape(1, CH)
            meansq = jnp.mean(conv * conv, axis=1, keepdims=True)
            normed = conv * lax.rsqrt(meansq + 1e-06) * gain_ref[...].reshape(1, CH)
            decoded = (normed / (1.0 + jnp.exp(-normed))).astype(BF16)
            for c in range(2):
                for f in range(FR):
                    out_ref[f, a, 2 * c + b] = decoded[c * 6 + f]


def body(
    queries,
    stretch_keys,
    stretch_values,
    cache_keys,
    cache_values,
    cache_lengths,
    frame_mask,
    out_weight,
    head_weight,
    previous_latent,
    conv_weight,
    conv_bias,
    norm_gain,
):
    z = lax.axis_index("z")
    vmem = pl.BlockSpec(memory_space=pltpu.VMEM)
    whole = pl.BlockSpec()
    hbm = pl.BlockSpec(memory_space=pltpu.HBM)
    smem = pl.BlockSpec(memory_space=pltpu.SMEM)

    def call(kernel, name, outs, specs, scratch=(), limit=16, **kw):
        shapes = [jax.ShapeDtypeStruct(shape, kind) for shape, kind in outs]
        return pl.pallas_call(
            kernel,
            out_shape=shapes if len(shapes) > 1 else shapes[0],
            in_specs=specs,
            out_specs=[vmem] * len(shapes) if len(shapes) > 1 else vmem,
            scratch_shapes=scratch,
            compiler_params=pltpu.CompilerParams(vmem_limit_bytes=limit * 1024 * 1024),
            name=name,
            **kw,
        )

    keep, give, raw, q = call(
        pack_kernel,
        "pack",
        (((528, HD), BF16), ((528, HD), BF16), ((528, 2 * HD), BF16), ((8, 8, 16, HD), BF16)),
        [hbm] * 6,
        [
            pltpu.VMEM((5, 128, 2 * HD), BF16),
            pltpu.SMEM((1,), jnp.int32),
            pltpu.SemaphoreType.DMA((6,)),
        ],
        limit=60,
    )(cache_lengths, queries, cache_keys, stretch_keys, cache_values, stretch_values)
    def swap(x):
        return lax.ppermute(x, "h", [(0, 1), (1, 0)])

    got = swap(give)
    far = lax.ppermute(
        raw,
        ("z", "mp"),
        [(16 * i + j, 16 * ((i + (2 if j % 2 == 0 else 14)) % NZ) + j) for i in range(NZ) for j in range(16)],
    )
    hw = lax.dynamic_slice_in_dim(head_weight, 160 * (z % 2), 160, 0)
    hw = lax.all_to_all(jnp.broadcast_to(hw[None], (16, 160, 64)), "mp", 0, 0, tiled=True)
    q, hw = lax.optimization_barrier((q, hw))
    q = lax.all_to_all(q, ("z", "h"), 0, 0, tiled=True, axis_index_groups=FAR)
    kv = call(
        pair_kernel,
        "pair",
        (((2, 560, HD), BF16),),
        [vmem] * 3 + [hbm],
        [
            pltpu.VMEM((HD, 5120), BF16),
            pltpu.VMEM((5120, 64), BF16),
            pltpu.SemaphoreType.DMA((4,)),
        ],
        limit=52,
        cost_estimate=pl.CostEstimate(flops=0, bytes_accessed=10**6, transcendentals=0),
    )(keep, got, hw, out_weight)
    up = lax.ppermute(kv, "z", [(i, (i + 1) % NZ) for i in range(NZ)])
    down = lax.ppermute(kv, "z", [((i + 1) % NZ, i) for i in range(NZ)])
    cost = pl.CostEstimate(flops=10**10, bytes_accessed=10**6, transcendentals=10**6)
    far_keep, far_give = call(
        split_kernel,
        "split",
        (((528, HD), BF16), ((528, HD), BF16)),
        [vmem],
        cost_estimate=pl.CostEstimate(flops=10**10, bytes_accessed=10**6, transcendentals=0),
    )(far)
    far_got = swap(far_give)
    first = call(
        first_kernel,
        "first",
        (((8, 128, HD), BF16), ((8, 8, 128), F32)),
        [smem] + [vmem] * 4,
        cost_estimate=cost,
    )(frame_mask, q, kv, far_keep, far_got)
    partial = call(
        second_kernel,
        "second",
        (((NZ, 48, 128), BF16),),
        [smem] + [vmem] * 7,
        [pltpu.VMEM((8, 64, 128), F32), pltpu.VMEM((8, 8, 128), F32)],
        cost_estimate=cost,
    )(frame_mask, q, kv, up, down, *first, previous_latent)
    partial = lax.all_to_all(partial, "z", 0, 0, tiled=True)
    spread = call(spread_kernel, "spread", (((32, 32, 128), BF16),), [vmem, whole], [pltpu.VMEM((16, 32, 128), F32)])(
        partial, previous_latent
    )
    spread = lax.all_to_all(spread, ("h", "mp"), 0, 0, tiled=True)
    return call(
        decode_kernel,
        "decode",
        (((FR, 2, 4, CH), BF16),),
        [vmem] + [whole] * 3,
        [pltpu.VMEM((2, 40, 64), F32), pltpu.VMEM((2, 2, 3, 256, CH), BF16)],
    )(spread, conv_weight, conv_bias, norm_gain)


def solution(mesh):
    fine = Mesh(mesh.devices.reshape(NZ, 2, 16), ("z", "h", "mp"))
    seq = ("z", "h")
    return jax.shard_map(
        body,
        mesh=fine,
        in_specs=(
            P(seq, "mp"),
            P(seq, "mp"),
            P(seq, "mp"),
            P(seq, "mp"),
            P(seq, "mp"),
            P(seq),
            P(),
            P("mp", None),
            P("mp", None),
            P(None, "mp", seq, None),
            P(),
            P(),
            P(),
        ),
        out_specs=P(None, "mp", seq, None),
        check_vma=False,
    )
```
